128 devices in a mesh: expert: 32 (over y, x, core), tensor: 4 (over z).
Axes of the slice: x: 4, y: 4, z: 4, core: 2. Of those that a mesh axis runs over, the one named last changes fastest.
Arguments:
- residual: bfloat16 [1024, 7168], P(('expert', 'tensor')), may hold values from -3 to 3
- query_latent: bfloat16 [512, 2, 32, 512], P(('expert', 'tensor')), may hold values from -48 to 48
- query_rope: bfloat16 [512, 2, 32, 64], P(('expert', 'tensor')), may hold values from -6 to 6
- cache_latent: bfloat16 [512, 2048, 512], P(('expert', 'tensor')), may hold values from -6 to 6
- cache_rope: bfloat16 [512, 64, 2048], P(('expert', 'tensor')), may hold values from -6 to 6
- new_latent: bfloat16 [512, 2, 512], P(('expert', 'tensor')), may hold values from -6 to 6
- new_rope: bfloat16 [512, 2, 64], P(('expert', 'tensor')), may hold values from -6 to 6
- lengths: int32 [512], P(('expert', 'tensor')), may hold values from 256 to 2048, as said below
- value_proj: bfloat16 [32, 512, 128], replicated, may hold values from -2.5 to 2.5
- out_proj: bfloat16 [4096, 7168], P(None, 'expert'), may hold values from -0.09375 to 0.09375
- norm_gain: bfloat16 [7168], replicated, may hold values from 0.099609375 to 1.8984375
- expert_ids: int32 [1024, 8], P(('expert', 'tensor')), may hold values from 0 to 31, all different within a row; in each aligned block of 8 rows (0 to 7, 8 to 15, ...) at most 4 rows name the same one
- expert_gates: float32 [1024, 8], P(('expert', 'tensor')), may hold values from 0.05 to 0.5
- w_gate: bfloat16 [32, 7168, 1024], P('expert', None, 'tensor'), may hold values from -0.0625 to 0.0625
- w_up: bfloat16 [32, 7168, 1024], P('expert', None, 'tensor'), may hold values from -0.0625 to 0.0625
- w_down: bfloat16 [32, 1024, 7168], P('expert', 'tensor'), may hold values from -0.1875 to 0.1875
Outputs:
- layer_out: bfloat16 [1024, 7168], P(('expert', 'tensor'))
The draws below stay inside these ranges and needn't reach their ends.
Inputs may be any that keep to these rules, and one draw needn't show every extreme that they name: `lengths`: some request's context holds all 2048 cached entries. `expert_ids`: among the rows of one device each expert is named at most 4 times.
All inputs are finite; a program needn't handle non-finite values.
Results may differ from the reference program's by a relative error of at most 0.012.
Values may be sent and summed in bfloat16 or wider, within the bound.
No kernel may reach another device: no remote copies, remote signals or barrier semaphores. Data moves between devices by JAX's collectives and lax.ppermute only.
A program may use at most 128 MiB of HBM per device.

```python
import math
import jax
import jax.numpy as jnp
import numpy as np
from jax import lax

D = 7168
HEADS = 32
LAT = 512
ROPE = 64
VDIM = 128
FF = 1024
TOPK = 8
STEPS = 2
CTX = 2048
EXPERTS = 32
REQUESTS = 512
TOK_DEV = 8
TOKENS = 1024
CAP = 4
N_EXPERT = 32
N_TENSOR = 4


def draw_cache_latent(key, part):
    key = jax.random.fold_in(key, 11)
    cache = jax.random.normal(key, (REQUESTS, CTX, LAT), jnp.float32)
    return jnp.clip(cache, -6.0, 6.0).astype(jnp.bfloat16)


def draw_query_latent(key, part):
    key = jax.random.fold_in(key, 12)
    noise_key = jax.random.fold_in(key, 0)
    query = jax.random.normal(noise_key, (REQUESTS, STEPS, HEADS, LAT), jnp.float32)
    return jnp.clip(query, -48.0, 48.0).astype(jnp.bfloat16)


def draw_lengths(key, part):
    key = jax.random.fold_in(key, 13)
    counts = jax.random.randint(key, (REQUESTS,), CTX // 8, CTX + 1)
    return counts.at[0].set(CTX).astype(jnp.int32)


def block_levels(rng, dims, cuts, smallest, top_value):
    def one(dim, parts):
        steps = jax.random.uniform(jax.random.fold_in(jax.random.fold_in(rng, 6), dim), (parts,), jnp.float32, smallest / len(cuts), top_value / len(cuts))
        return jnp.repeat(jnp.exp(steps), dims[dim] // parts).reshape((-1,) + (1,) * (len(dims) - dim - 1))

    factor_of = one(*cuts[0])
    for cut in cuts[1:]:
        factor_of = factor_of * one(*cut)
    return factor_of


def routed_block(rng, own, number, rows, amount, top, reach, skew):
    order = jax.random.permutation(rng, amount)
    packed, usual = load_shares(amount, rows * top, reach, skew, True), load_shares(amount, rows * top, reach, skew, False)
    places = jnp.arange(amount)

    def named(sizes, turn):
        used = int((sizes > 0).sum())
        fixed = max(1, used // 4)
        passed = fixed + (places - fixed + turn * (used - fixed)) % max(1, amount - fixed)
        return jnp.zeros((amount,), jnp.int32).at[order[jnp.where(places < fixed, places, passed)]].set(jnp.asarray(sizes, jnp.int32))

    sizes = jnp.where(number % 4 == 0, named(packed, number // 4), named(usual, number - number // 4 - 1))
    mixed = jax.random.permutation(jax.random.fold_in(own, 3), amount)
    giver, receiver = mixed[0:amount // 2 * 2:2], mixed[1:amount // 2 * 2:2]
    room = jnp.minimum(sizes[giver] - 1, reach - sizes[receiver]) // 2
    room = jnp.where((giver == order[0]) | (receiver == order[0]) | (sizes[receiver] == 0), 0, jnp.maximum(room, 0))
    passed = jax.random.randint(jax.random.fold_in(own, 4), (amount // 2,), 0, 1 << 20) % (room + 1)
    sizes = sizes.at[giver].add(-passed).at[receiver].add(passed)
    members = jnp.searchsorted(jnp.cumsum(sizes), jnp.arange(rows * top), side="right").astype(jnp.int32)
    grid = members.reshape(top, rows).T
    grid = grid[jax.random.permutation(jax.random.fold_in(own, 1), rows)]
    turn = jax.random.randint(jax.random.fold_in(own, 2), (rows, 1), 0, top)
    return jnp.take_along_axis(grid, (jnp.arange(top)[None, :] + turn) % top, axis=1)


def load_shares(amount, total, most, skew, full):
    weights = [(1 << 20) // math.isqrt(rank ** skew) + 1 for rank in range(1, amount + 1)]
    largest = most if full else min(most, max(-(-total // amount), total * weights[0] // sum(weights)))
    least = 1 if total - largest >= amount - 1 else 0
    given, surplus = [largest] + [least] * (amount - 1), total - largest - least * (amount - 1)
    while surplus > 0:
        candidates = [i for i in range(1, amount) if given[i] < largest] or [i for i in range(1, amount) if given[i] < most]
        pool, left = sum([weights[i] for i in candidates]), surplus
        for i in candidates:
            addition = min(most - given[i], max(1, left * weights[i] // pool), surplus)
            given[i] = given[i] + addition
            surplus = surplus - addition
    return np.array(given)


def noise(key, shape, scale, limit, cuts=(), kind=jnp.bfloat16):
    gain = block_levels(key, shape, cuts, -0.22, 0.18) if cuts else 1.0
    drawn = jax.random.normal(key, shape, jnp.float32) * scale * gain
    return jnp.minimum(jnp.maximum(drawn, -limit), limit).astype(kind)


def setup_inputs(seed: int = 0) -> dict:
    arg_keys = jax.random.split(jax.random.key(seed), 17)
    residual = noise(arg_keys[0], (TOKENS, D), 0.5, 3.0, ((0, 128),))
    query_latent = draw_query_latent(jax.random.fold_in(arg_keys[16], 71), 0)
    query_rope = noise(arg_keys[2], (REQUESTS, STEPS, HEADS, ROPE), 1.0, 6.0, ((0, 128),))
    cache_latent = draw_cache_latent(jax.random.fold_in(arg_keys[16], 71), 0)
    cache_rope = noise(arg_keys[4], (REQUESTS, ROPE, CTX), 1.0, 6.0, ((0, 128),))
    new_latent = noise(arg_keys[5], (REQUESTS, STEPS, LAT), 1.0, 6.0, ((0, 128),))
    new_rope = noise(arg_keys[6], (REQUESTS, STEPS, ROPE), 1.0, 6.0, ((0, 128),))
    lengths = draw_lengths(jax.random.fold_in(arg_keys[16], 71), 0)
    value_proj = noise(arg_keys[8], (HEADS, LAT, VDIM), (4.0 * LAT ** -0.5), 2.5)
    out_proj = noise(arg_keys[9], (HEADS * VDIM, D), (HEADS * VDIM) ** -0.5, 0.09375, ((1, 32),))
    norm_gain = jnp.clip(1.0 + 0.18 * jax.random.normal(arg_keys[10], (D,), jnp.float32), 0.099609375, 1.8984375).astype(jnp.bfloat16)
    expert_ids_keys = jax.random.split(jax.random.fold_in(arg_keys[11], 1), TOKENS // TOK_DEV)
    expert_ids_turns = jax.random.permutation(jax.random.fold_in(arg_keys[11], 3), TOKENS // TOK_DEV)
    expert_ids = jax.vmap(lambda own, number: routed_block(jax.random.fold_in(arg_keys[11], 2), own, number, TOK_DEV, EXPERTS, TOPK, CAP, 2))(expert_ids_keys, expert_ids_turns).reshape((TOKENS, TOPK))
    expert_gates = jnp.clip(jnp.exp(math.log(0.5) - 2.3025851 * jax.random.uniform(arg_keys[12], (TOKENS, TOPK), jnp.float32) ** block_levels(arg_keys[12], (TOKENS, TOPK), ((0, 128),), -0.2, 0.2)), 0.05, 0.5)
    w_gate = noise(arg_keys[13], (EXPERTS, D, FF), D ** -0.5, 0.0625, ((0, 32), (2, 4)))
    w_up = noise(arg_keys[14], (EXPERTS, D, FF), D ** -0.5, 0.0625, ((0, 32), (2, 4)))
    w_down = noise(arg_keys[15], (EXPERTS, FF, D), FF ** -0.5, 0.1875, ((0, 32), (1, 4)))
    return dict(residual=residual, query_latent=query_latent, query_rope=query_rope, cache_latent=cache_latent, cache_rope=cache_rope, new_latent=new_latent, new_rope=new_rope, lengths=lengths, value_proj=value_proj, out_proj=out_proj, norm_gain=norm_gain, expert_ids=expert_ids, expert_gates=expert_gates, w_gate=w_gate, w_up=w_up, w_down=w_down)


EPSILON = 1e-06

def attend_request(operands):
    q_lat, q_rope, latent, rope_keys, fresh_latent, fresh_rope, length = operands
    score_scale = (VDIM + ROPE) ** (-0.5)
    cached = jnp.einsum('shl,cl->shc', q_lat.astype(jnp.float32), latent.astype(jnp.float32))
    cached = cached + jnp.einsum('shp,pc->shc', q_rope.astype(jnp.float32), rope_keys.astype(jnp.float32))
    recent = jnp.einsum('shl,nl->shn', q_lat.astype(jnp.float32), fresh_latent.astype(jnp.float32))
    recent = recent + jnp.einsum('shp,np->shn', q_rope.astype(jnp.float32), fresh_rope.astype(jnp.float32))
    cache_valid = jnp.arange(CTX, dtype=jnp.int32) < length
    recent_valid = jnp.arange(STEPS, dtype=jnp.int32)[None, :] <= jnp.arange(STEPS, dtype=jnp.int32)[:, None]
    cached = jnp.where(cache_valid[None, None, :], cached * score_scale, -1e+30)
    recent = jnp.where(recent_valid[:, None, :], recent * score_scale, -1e+30)
    scores = jnp.concatenate([cached, recent], axis=-1)
    weights = jax.nn.softmax(scores, axis=-1).astype(jnp.bfloat16)
    mixed = jnp.einsum('shc,cl->shl', weights[..., :CTX].astype(jnp.float32), latent.astype(jnp.float32))
    mixed = mixed + jnp.einsum('shn,nl->shl', weights[..., CTX:].astype(jnp.float32), fresh_latent.astype(jnp.float32))
    return mixed.astype(jnp.bfloat16)

def reference(residual, query_latent, query_rope, cache_latent, cache_rope, new_latent, new_rope, lengths, value_proj, out_proj, norm_gain, expert_ids, expert_gates, w_gate, w_up, w_down):
    mixed = lax.map(attend_request, (query_latent, query_rope, cache_latent, cache_rope, new_latent, new_rope, lengths))
    head_values = jnp.einsum('rshl,hlv->rshv', mixed.astype(jnp.float32), value_proj.astype(jnp.float32))
    head_values = head_values.astype(jnp.bfloat16).reshape(TOKENS, HEADS * VDIM)
    attn_out = jnp.dot(head_values, out_proj, preferred_element_type=jnp.float32).astype(jnp.bfloat16)
    stream = residual.astype(jnp.float32) + attn_out.astype(jnp.float32)
    inverse = lax.rsqrt(lax.optimization_barrier(jnp.mean(stream * stream, axis=-1, keepdims=True)) + EPSILON)
    normed = (stream * inverse * norm_gain.astype(jnp.float32)).astype(jnp.bfloat16)
    devices_all = N_EXPERT * N_TENSOR
    assigned = TOK_DEV * TOPK
    per_device = expert_ids.reshape(devices_all, assigned).astype(jnp.int32)
    expert_hot = (per_device[..., None] == jnp.arange(EXPERTS, dtype=jnp.int32)).astype(jnp.int32)
    slot_index = lax.optimization_barrier(jnp.sum(expert_hot * (jnp.cumsum(expert_hot, axis=1) - 1), axis=-1)).astype(jnp.int32)
    device_index = jnp.broadcast_to(jnp.arange(devices_all, dtype=jnp.int32)[:, None], (devices_all, assigned))
    token_index = (device_index * TOK_DEV + jnp.arange(assigned, dtype=jnp.int32)[None, :] // TOPK).astype(jnp.int32)
    table = jnp.full((EXPERTS, devices_all, CAP), TOKENS, jnp.int32)
    table = table.at[per_device, device_index, slot_index].set(token_index)
    gate_table = jnp.zeros((EXPERTS, devices_all, CAP), jnp.float32)
    gate_table = gate_table.at[per_device, device_index, slot_index].set(expert_gates.reshape(devices_all, assigned).astype(jnp.float32))
    padded = jnp.concatenate([normed, jnp.zeros((1, D), jnp.bfloat16)], axis=0)
    share = FF // N_TENSOR

    def expert_step(total, operands):
        gate_w, up_w, down_w, rows_index, row_gates = operands
        flat_index = rows_index.reshape(-1)
        rows = padded[flat_index]
        gate_act = jnp.dot(rows, gate_w, preferred_element_type=jnp.float32)
        up_act = jnp.dot(rows, up_w, preferred_element_type=jnp.float32)
        hidden = (jax.nn.silu(gate_act) * up_act).astype(jnp.bfloat16)
        summed = jnp.zeros((rows.shape[0], D), jnp.float32)
        for group in range(N_TENSOR):
            piece = jnp.dot(hidden[:, group * share:(group + 1) * share], down_w[group * share:(group + 1) * share], preferred_element_type=jnp.float32).astype(jnp.bfloat16)
            summed = summed + lax.optimization_barrier(piece).astype(jnp.float32)
        result = summed.astype(jnp.bfloat16)
        result = lax.optimization_barrier(result).astype(jnp.float32)
        return (total.at[flat_index].add(row_gates.reshape(-1)[:, None] * result), None)
    total, _ = lax.scan(expert_step, jnp.zeros((TOKENS + 1, D), jnp.float32), (w_gate, w_up, w_down, table, gate_table))
    return (stream + total[:TOKENS]).astype(jnp.bfloat16)
```

```python
import functools

import jax
import jax.numpy as jnp
from jax import lax
from jax.experimental import pallas as pl
from jax.experimental.pallas import tpu as pltpu
from jax.sharding import PartitionSpec as P

EPSILON = 1e-06
BOTH = ("expert", "tensor")
SIDE = 4
CHIPS = 16
ROWS_A, ROWS_B, ROWS_C = 336, 352, 336
F32 = jnp.float32
BF16 = jnp.bfloat16


def expert_of(y, x, core):
    return (y * SIDE + x) * 2 + core


def masks_of(core):
    return (1, 3) if core == 0 else (3, 1)


def swap_core(value):
    pairs = [(e, e ^ 1) for e in range(2 * CHIPS)]
    return lax.ppermute(value, "expert", pairs)


def shift_z(value, amount):
    pairs = [(z, (z + amount) % SIDE) for z in range(SIDE)]
    return lax.ppermute(value, "tensor", pairs)


def exchange(value, axis, turn):
    pairs = []
    for y in range(SIDE):
        for x in range(SIDE):
            for core in range(2):
                mask = masks_of(core)[turn]
                here = expert_of(y, x, core)
                if axis == "x":
                    pairs.append((here, expert_of(y, x ^ mask, core)))
                elif axis == "y":
                    pairs.append((here, expert_of(y ^ mask, x, core)))
                else:
                    for z in range(SIDE):
                        pairs.append((here * SIDE + z, here * SIDE + (z ^ mask)))
    return lax.ppermute(value, BOTH if axis == "z" else "expert", pairs)


def after(first, *later):
    return lax.optimization_barrier((first[-8:, :128], *later))[1:]


def grow(value, axis, turn):
    return jnp.concatenate([value, exchange(value, axis, turn)], axis=0)


def attend_kernel(length_ref, q_ref, qr_ref, latent_ref, rope_ref, fresh_ref, fresh_rope_ref, out_ref, *, scale, heads):
    request = pl.program_id(0)
    query = q_ref[0]
    query_rope = qr_ref[0]
    latent = latent_ref[0]
    last = (((1,), (1,)), ((), ()))
    scores = lax.dot_general(query, latent, last, preferred_element_type=F32)
    scores = scores + jnp.dot(query_rope, rope_ref[0], preferred_element_type=F32)
    lane = lax.broadcasted_iota(jnp.int32, (1, scores.shape[1]), 1)
    scores = jnp.where(lane < length_ref[request], scores * scale, -1e30)
    fresh = fresh_ref[0]
    fresh_rope = fresh_rope_ref[0]
    recent = lax.dot_general(query, fresh, last, preferred_element_type=F32)
    recent = recent + lax.dot_general(query_rope, fresh_rope, last, preferred_element_type=F32)
    step = lax.broadcasted_iota(jnp.int32, recent.shape, 0) // heads
    place = lax.broadcasted_iota(jnp.int32, recent.shape, 1)
    recent = jnp.where(place <= step, recent * scale, -1e30)
    top = jnp.maximum(
        jnp.max(scores, axis=1, keepdims=True), jnp.max(recent, axis=1, keepdims=True)
    )
    weights = jnp.exp(scores - top)
    recent = jnp.exp(recent - top)
    total = jnp.sum(weights, axis=1, keepdims=True) + jnp.sum(recent, axis=1, keepdims=True)
    share = 1.0 / total
    mixed = jnp.dot((weights * share).astype(BF16), latent, preferred_element_type=F32)
    recent = (recent * share).astype(BF16).astype(F32)
    for n in range(fresh.shape[0]):
        mixed = mixed + recent[:, n : n + 1] * fresh[n : n + 1].astype(F32)
    out_ref[0] = mixed.astype(BF16)


def attention_heads(
    query_latent, query_rope, cache_latent, cache_rope, new_latent, new_rope, lengths, value_proj
):
    requests, steps, heads, latent = query_latent.shape
    rope = query_rope.shape[3]
    context = cache_latent.shape[1]
    rows = steps * heads
    scale = (value_proj.shape[2] + rope) ** (-0.5)
    whole = lambda *shape: pl.BlockSpec((1,) + shape, lambda i, s: (i, 0, 0))
    mixed = pl.pallas_call(
        functools.partial(attend_kernel, scale=scale, heads=heads),
        grid_spec=pltpu.PrefetchScalarGridSpec(
            num_scalar_prefetch=1,
            grid=(requests,),
            in_specs=[
                whole(rows, latent),
                whole(rows, rope),
                whole(context, latent),
                whole(rope, context),
                whole(steps, latent),
                whole(steps, rope),
            ],
            out_specs=whole(rows, latent),
        ),
        out_shape=jax.ShapeDtypeStruct((requests, rows, latent), BF16),
        cost_estimate=pl.CostEstimate(
            flops=2 * requests * rows * context * (2 * latent + rope),
            bytes_accessed=2 * requests * context * (latent + rope),
            transcendentals=requests * rows * context,
        ),
        compiler_params=pltpu.CompilerParams(vmem_limit_bytes=56 << 20),
    )(
        lengths,
        query_latent.reshape(requests, rows, latent),
        query_rope.reshape(requests, rows, rope),
        cache_latent,
        cache_rope,
        new_latent,
        new_rope,
    )
    head_values = jnp.einsum(
        "rshl,hlv->rshv",
        mixed.reshape(requests, steps, heads, latent),
        value_proj,
        preferred_element_type=F32,
    )
    return head_values.astype(BF16).reshape(requests * steps, -1)


def pack_kernel(heads_ref, residual_ref, routing_ref, out_ref):
    width = heads_ref.shape[1]
    cols = residual_ref.shape[1] // CHIPS
    for chip in range(CHIPS):
        out_ref[chip, :, :width] = heads_ref[...]
        part = residual_ref[:, chip * cols : (chip + 1) * cols]
        out_ref[chip, :, width:] = jnp.concatenate([part, routing_ref[chip]], axis=1)


def pack(heads, residual, routing):
    rows, width = heads.shape
    cols = residual.shape[1] // CHIPS
    routing = jnp.pad(routing, ((0, 0), (0, 0), (0, 512 - cols - routing.shape[2])))
    return pl.pallas_call(
        pack_kernel,
        out_shape=jax.ShapeDtypeStruct((CHIPS, rows, width + 512), BF16),
        cost_estimate=pl.CostEstimate(
            flops=0, bytes_accessed=2 * CHIPS * rows * (width + 512), transcendentals=0
        ),
    )(heads, residual, routing)


def project_kernel(
    place_ref, in_ref, own_ref, other_ref, gain_ref, out_ref, sum_own, sum_other, *, width
):
    step = pl.program_id(0)
    depth = own_ref.shape[1]

    @pl.when(step == 0)
    def _():
        sum_own[...] = jnp.zeros_like(sum_own)
        sum_other[...] = jnp.zeros_like(sum_other)

    heads = in_ref[:, pl.ds(pl.multiple_of(step * depth, 128), depth)]
    dims = (((1,), (1,)), ((), ()))
    sum_own[...] += lax.dot_general(heads, own_ref[...], dims, preferred_element_type=F32)
    sum_other[...] += lax.dot_general(heads, other_ref[...], dims, preferred_element_type=F32)

    @pl.when(step == pl.num_programs(0) - 1)
    def _():
        first = place_ref[0] == 0
        own, other = sum_own[...], sum_other[...]
        left = jnp.where(first, own, other)
        right = jnp.where(first, other, own)
        both = jnp.concatenate([left, right], axis=1).astype(BF16).astype(F32)
        tail = in_ref[:, width:].astype(F32)
        cols = both.shape[1]
        stream = tail[:, :cols] + both
        square = jnp.sum(stream * stream, axis=1, keepdims=True)
        high = square.astype(BF16).astype(F32)
        low = square - high
        extra = tail[:, cols:]
        lane = lax.broadcasted_iota(jnp.int32, extra.shape, 1)
        extra = jnp.where(lane == 6, high, jnp.where(lane == 7, low, extra))
        stream = stream * gain_ref[0].astype(F32)
        out_ref[...] = jnp.concatenate([stream, extra], axis=1).astype(BF16)


def project(place, landed, own, other, gain):
    rows, total = landed.shape
    cols, width = own.shape
    steps = 4
    depth = width // steps
    out = total - width
    return pl.pallas_call(
        functools.partial(project_kernel, width=width),
        grid_spec=pltpu.PrefetchScalarGridSpec(
            num_scalar_prefetch=1,
            grid=(steps,),
            in_specs=[
                pl.BlockSpec((rows, total), lambda i, s: (0, 0)),
                pl.BlockSpec((cols, depth), lambda i, s: (0, i)),
                pl.BlockSpec((cols, depth), lambda i, s: (0, i)),
                pl.BlockSpec((1, 1, 2 * cols), lambda i, s: (s[1], 0, 0)),
            ],
            out_specs=pl.BlockSpec((rows, out), lambda i, s: (0, 0)),
            scratch_shapes=[pltpu.VMEM((rows, cols), F32)] * 2,
        ),
        out_shape=jax.ShapeDtypeStruct((rows, out), BF16),
        cost_estimate=pl.CostEstimate(
            flops=4 * rows * width * cols, bytes_accessed=4 * width * cols, transcendentals=0
        ),
        compiler_params=pltpu.CompilerParams(vmem_limit_bytes=24 << 20),
    )(place, landed, own, other, gain.reshape(CHIPS, 1, 2 * cols))


def hidden_kernel(
    place_ref,
    a0_ref,
    a1_ref,
    b0_ref,
    b1_ref,
    c0_ref,
    c1_ref,
    wg_ref,
    wgo_ref,
    wu_ref,
    wuo_ref,
    hidden_ref,
    index_ref,
    own_ref,
    tokens,
    weight,
    total,
    extras,
    named,
    arrived,
    *,
    model,
):
    far_y, far_x = pl.program_id(0), pl.program_id(1)
    step = far_y * 2 + far_x
    wide = a0_ref.shape[-1]
    cols = model // CHIPS
    part = wg_ref.shape[1]

    def fetch(at, near):
        source = pl.ds(pl.multiple_of(place_ref[at * 4 + near] * cols, 64), cols)
        return [
            pltpu.make_async_copy(
                ref.at[source],
                weight.at[at, pl.ds(near * wide, cols), pl.ds(i * part, part)],
                arrived.at[at, near, i],
            )
            for i, ref in enumerate((wg_ref, wgo_ref, wu_ref, wuo_ref))
        ]

    @pl.when(step == 0)
    def _():
        total[...] = jnp.zeros_like(total)
        extras[...] = jnp.zeros_like(extras)
        for at in range(4):
            for near in range(4):
                for copy in fetch(at, near):
                    copy.start()
        for at in range(4):
            for near in range(4):
                weight[at, near * wide + cols : (near + 1) * wide] = jnp.zeros(
                    (wide - cols, weight.shape[2]), BF16
                )

    def place_rows(far_z, first, value):
        start = 0
        while start < value.shape[0]:
            row = first + start
            count = min(128 - row % 128, value.shape[0] - start)
            near_z, near = divmod(row // 128, 4)
            at = (far_z * 2 + near_z) * 128 + row % 128
            tokens[at : at + count, near * wide : (near + 1) * wide] = value[start : start + count]
            start += count

    place_rows(0, 0, a0_ref[0])
    place_rows(1, 0, a1_ref[0])
    for bit, ref in ((0, b0_ref), (1, b1_ref)):

        @pl.when(far_x == bit)
        def _(ref=ref):
            place_rows(0, ROWS_A, ref[0, 0])
            place_rows(1, ROWS_A, ref[1, 0])

    for bit, ref in ((0, c0_ref), (1, c1_ref)):

        @pl.when(far_y == bit)
        def _(ref=ref):
            place_rows(0, ROWS_A + ROWS_B, ref[0, 0])
            place_rows(1, ROWS_A + ROWS_B, ref[0, 1])

    for near in range(4):
        for copy in fetch(step, near):
            copy.wait()
    total[...] += jnp.dot(tokens[...], weight[step], preferred_element_type=F32)

    @pl.when(step == 0)
    def _():
        named[...] = tokens[:, cols:wide].astype(F32)

    chip = place_ref[20]
    start = pl.multiple_of((chip // 2) * 16, 16)
    for near in range(4):
        extras[...] += tokens[:, near * wide + cols : (near + 1) * wide].astype(F32)
        mine = tokens[pl.ds(start, 16), near * wide : (near + 1) * wide].astype(F32)
        own_ref[pl.ds(place_ref[step * 4 + near], 1)] = jnp.where(
            lax.rem(chip, 2) == 0, mine[:8], mine[8:]
        )[None]

    @pl.when(step == 3)
    def _():
        sums = extras[...]
        square = (sums[:, 6:7] + sums[:, 7:8]) * (1.0 / model)
        inverse = lax.rsqrt(square + EPSILON)
        names = named[...]
        group = lax.broadcasted_iota(jnp.int32, (128, 1), 0) // 8
        bases = jnp.concatenate(
            [group * 4 + place_ref[16 + i] * (4 * CHIPS) for i in range(4)], axis=0
        )
        slots = bases.shape[0] // 2
        lanes = lax.broadcasted_iota(jnp.int32, (1, slots), 1)
        even = place_ref[21] == 0
        gates = [names[:, 2 * i : 2 * i + 1] + names[:, 2 * i + 1 : 2 * i + 2] for i in range(2)]
        ranks = [names[:, 4 + i : 5 + i].astype(jnp.int32) for i in range(2)]
        for i in range(2):
            gate = total[:, i * part : (i + 1) * part] * inverse
            up = total[:, (2 + i) * part : (3 + i) * part] * inverse
            share = jnp.where(even, gates[i], gates[1 - i])
            rank = jnp.where(even, ranks[i], ranks[1 - i])
            value = gate * (1.0 / (1.0 + jnp.exp(-gate))) * up * share
            place_index = jnp.where(rank < 4, bases + rank, -1)
            index_ref[:, i : i + 1] = place_index
            hot = (place_index == lanes).astype(BF16)
            hidden_ref[i] = lax.dot_general(
                hot, value.astype(BF16), (((0,), (0,)), ((), ())), preferred_element_type=F32
            ).astype(BF16)


def hidden_values(place, parts, weights):
    (a0, a1), (b0, b1), (c0, c1) = parts
    wide = a0.shape[-1]
    model, part = weights[0].shape
    cols = model // CHIPS
    tok = SIDE * 128
    a0, a1 = (v.reshape(4, ROWS_A, wide) for v in (a0, a1))
    b0, b1 = (v.reshape(2, 2, ROWS_B, wide) for v in (b0, b1))
    c0, c1 = (v.reshape(2, 2, ROWS_C, wide) for v in (c0, c1))
    a_spec = pl.BlockSpec((1, ROWS_A, wide), lambda y, x, s: (y * 2 + x, 0, 0))
    b_spec = pl.BlockSpec((2, 1, ROWS_B, wide), lambda y, x, s: (0, y, 0, 0))
    c_spec = pl.BlockSpec((1, 2, ROWS_C, wide), lambda y, x, s: (x, 0, 0, 0))
    return pl.pallas_call(
        functools.partial(hidden_kernel, model=model),
        grid_spec=pltpu.PrefetchScalarGridSpec(
            num_scalar_prefetch=1,
            grid=(2, 2),
            in_specs=[a_spec] * 2
            + [b_spec] * 2
            + [c_spec] * 2
            + [pl.BlockSpec(memory_space=pltpu.HBM)] * 4,
            out_specs=[
                pl.BlockSpec((2, tok // 2, part), lambda y, x, s: (0, 0, 0)),
                pl.BlockSpec((tok, 2), lambda y, x, s: (0, 0)),
                pl.BlockSpec((CHIPS, 8, wide), lambda y, x, s: (0, 0, 0)),
            ],
            scratch_shapes=[
                pltpu.VMEM((tok, 4 * wide), BF16),
                pltpu.VMEM((4, 4 * wide, 4 * part), BF16),
                pltpu.VMEM((tok, 4 * part), F32),
                pltpu.VMEM((tok, wide - cols), F32),
                pltpu.VMEM((tok, wide - cols), F32),
                pltpu.SemaphoreType.DMA((4, 4, 4)),
            ],
        ),
        out_shape=[
            jax.ShapeDtypeStruct((2, tok // 2, part), BF16),
            jax.ShapeDtypeStruct((tok, 2), jnp.int32),
            jax.ShapeDtypeStruct((CHIPS, 8, wide), F32),
        ],
        cost_estimate=pl.CostEstimate(
            flops=8 * tok * CHIPS * wide * part,
            bytes_accessed=8 * model * part + 2 * tok * CHIPS * wide,
            transcendentals=2 * tok * part,
        ),
        compiler_params=pltpu.CompilerParams(vmem_limit_bytes=50 << 20),
    )(place, a0, a1, b0, b1, c0, c1, *weights)


def down_kernel(place_ref, index_ref, *refs):
    hidden, weights, (out_ref, spread) = refs[:4], refs[4:12], refs[12:]
    slots, part = hidden[0].shape[1:]

    @pl.when(pl.program_id(0) == 0)
    def _():
        lanes = lax.broadcasted_iota(jnp.int32, (1, slots), 1)
        for i in range(2):
            hot = (index_ref[:, i : i + 1] == lanes).astype(BF16)
            for k, ref in enumerate(hidden):
                at = (i * 4 + k) * part
                spread[:, at : at + part] = jnp.dot(
                    hot, ref[i], preferred_element_type=F32
                ).astype(BF16)

    weight = jnp.concatenate([ref[...] for ref in weights], axis=0)
    total = jnp.dot(spread[...], weight, preferred_element_type=F32).astype(BF16)
    for i in range(4):
        start = pl.multiple_of(place_ref[16 + i] * 128, 128)
        out_ref[pl.ds(start, 128), :] = total[i * 128 : (i + 1) * 128]


def down(place, index, hidden, own, other):
    tok = index.shape[0]
    slots, part = hidden[0].shape[1:]
    width = own[1].shape[1]
    tile = width // 2
    h_spec = pl.BlockSpec((2, slots, part), lambda i, s: (0, 0, 0))
    return pl.pallas_call(
        down_kernel,
        grid_spec=pltpu.PrefetchScalarGridSpec(
            num_scalar_prefetch=1,
            grid=(width // tile,),
            in_specs=[pl.BlockSpec((tok, 2), lambda i, s: (0, 0))]
            + [h_spec] * 4
            + [
                pl.BlockSpec((part, tile), lambda i, s: (0, s[22] * 2 + i)),
            ]
            + [pl.BlockSpec((part, tile), lambda i, s: (0, i))] * 7,
            out_specs=pl.BlockSpec((tok, tile), lambda i, s: (0, i)),
            scratch_shapes=[pltpu.VMEM((tok, 8 * part), BF16)],
        ),
        out_shape=jax.ShapeDtypeStruct((tok, width), BF16),
        cost_estimate=pl.CostEstimate(
            flops=16 * tok * part * width, bytes_accessed=16 * part * width, transcendentals=0
        ),
        compiler_params=pltpu.CompilerParams(vmem_limit_bytes=48 << 20),
    )(place, index, *hidden, *own, *other)


def routing_columns(expert_ids, expert_gates):
    rows, count = expert_ids.shape
    experts = 2 * CHIPS
    hot = expert_ids[:, :, None] == jnp.arange(experts, dtype=jnp.int32)
    gates = jnp.sum(jnp.where(hot, expert_gates[:, :, None], 0.0), axis=1)
    named = jnp.any(hot, axis=1)
    ones = named.astype(F32)
    below = jnp.tril(jnp.ones((rows, rows), F32), -1)
    rank = jnp.where(named, jnp.sum(below[:, :, None] * ones[None], axis=1), 8.0)
    high = lax.reduce_precision(gates, 8, 7)
    low = gates - high
    pair = lambda v: v.reshape(rows, CHIPS, 2).transpose(1, 0, 2)
    gate_pair = jnp.stack([pair(high), pair(low)], axis=-1).reshape(CHIPS, rows, 4)
    return jnp.concatenate([gate_pair, pair(rank)], axis=-1).astype(BF16)


def per_device(
    residual,
    query_latent,
    query_rope,
    cache_latent,
    cache_rope,
    new_latent,
    new_rope,
    lengths,
    value_proj,
    out_proj,
    norm_gain,
    expert_ids,
    expert_gates,
    w_gate,
    w_up,
    w_down,
):
    rows, model = residual.shape
    expert = lax.axis_index("expert")
    plane = lax.axis_index("tensor")
    core = expert % 2
    chip = expert // 2
    first = jnp.where(core == 0, 1, 3)
    second = 4 - first
    table = []
    for far_y in range(2):
        for far_x in range(2):
            for near_y in range(2):
                for near_x in range(2):
                    mask_x = (first * near_x) ^ (second * far_x)
                    mask_y = (first * near_y) ^ (second * far_y)
                    table.append(chip ^ (mask_y * SIDE + mask_x))
    for far_z in range(2):
        for near_z in range(2):
            table.append(plane ^ ((first * near_z) ^ (second * far_z)))
    table += [chip, core, plane, chip]
    place = jnp.stack([jnp.asarray(v, jnp.int32) for v in table])

    quarter = model // SIDE
    half = w_down.shape[1]
    cut = lambda v, z: lax.dynamic_slice(v, (0, z * quarter), (half, quarter))
    lengths, passed = lax.optimization_barrier((lengths, cut(w_down[0], plane ^ first ^ second)))
    passed = exchange(passed, "z", 0)
    out_own = out_proj.T
    out_other = swap_core(out_own)
    gate_own, up_own = w_gate[0], w_up[0]
    gate_other, up_other = swap_core(gate_own), swap_core(up_own)

    heads = attention_heads(
        query_latent,
        query_rope,
        cache_latent,
        cache_rope,
        new_latent,
        new_rope,
        lengths,
        value_proj,
    )
    cols = model // CHIPS
    sent = pack(heads, residual, routing_columns(expert_ids, expert_gates))
    sent, out_other, gate_other, up_other, passed, late_down = lax.optimization_barrier(
        (sent, out_other, gate_other, up_other, passed, w_down[0])
    )
    near = exchange(cut(late_down, plane ^ first), "z", 0)
    far = exchange(cut(late_down, plane ^ second), "z", 1)
    lane_plane = [
        [expert_of(y, x, core) for y in range(SIDE) for x in range(SIDE)] for core in range(2)
    ]
    landed = lax.all_to_all(
        sent, "expert", split_axis=0, concat_axis=0, tiled=True, axis_index_groups=lane_plane
    )
    landed, near, far = lax.optimization_barrier((landed, near, far))
    block = project(
        jnp.stack([core, chip]).astype(jnp.int32),
        landed.reshape(CHIPS * rows, -1),
        out_own,
        out_other,
        norm_gain,
    )
    block = grow(block, "x", 0)
    block = grow(block, "y", 0)
    block = grow(block, "z", 0)
    part_a = block[:ROWS_A]
    part_b = block[ROWS_A : ROWS_A + ROWS_B]
    part_c = block[ROWS_A + ROWS_B :]
    part_a, part_b, part_c = grow(part_a, "x", 1), grow(part_b, "y", 1), grow(part_c, "z", 1)
    part_a, part_b, part_c = grow(part_a, "y", 1), grow(part_b, "z", 1), grow(part_c, "x", 1)
    late_down, near_sent, far_sent = after(part_a, w_down[0], near, far)
    first_other = swap_core(cut(late_down, plane))
    near_other, far_other = swap_core(near_sent), swap_core(far_sent)
    parts = (
        (part_a, exchange(part_a, "z", 1)),
        (part_b, exchange(part_b, "x", 1)),
        (part_c, exchange(part_c, "y", 1)),
    )
    (passed,) = after(parts[2][1], passed)
    last = exchange(passed, "z", 1)
    hidden, index, own = hidden_values(
        place, parts, (gate_own, gate_other, up_own, up_other)
    )
    index, last = lax.optimization_barrier((index, last))
    last_other = swap_core(last)
    spread = [hidden, exchange(hidden, "z", 0), exchange(hidden, "z", 1), shift_z(hidden, 2)]
    sums = down(
        place,
        index,
        spread,
        (w_down[0], near, far, last),
        (first_other, far_other, near_other, last_other),
    )
    lane_all = [
        [expert_of(y, x, core) * SIDE + z for z in range(SIDE) for y in range(SIDE) for x in range(SIDE)]
        for core in range(2)
    ]
    returned = lax.all_to_all(
        sums.reshape(SIDE * CHIPS, rows, quarter),
        BOTH,
        split_axis=0,
        concat_axis=0,
        tiled=True,
        axis_index_groups=lane_all,
    )
    routed = jnp.sum(returned.reshape(SIDE, CHIPS, rows, quarter).astype(F32), axis=1)
    routed = routed.transpose(1, 0, 2).reshape(rows, model)
    stream = own[:, :, :cols].transpose(1, 0, 2).reshape(rows, model) / norm_gain.astype(F32)
    return (stream + routed).astype(BF16)


def solution(mesh):
    return jax.shard_map(
        per_device,
        mesh=mesh,
        in_specs=(
            P(BOTH, None),
            P(BOTH, None, None, None),
            P(BOTH, None, None, None),
            P(BOTH, None, None),
            P(BOTH, None, None),
            P(BOTH, None, None),
            P(BOTH, None, None),
            P(BOTH),
            P(),
            P(None, "expert"),
            P(),
            P(BOTH, None),
            P(BOTH, None),
            P("expert", None, "tensor"),
            P("expert", None, "tensor"),
            P("expert", "tensor", None),
        ),
        out_specs=P(BOTH, None),
        check_vma=False,
    )
```

```python
import functools

import jax
import jax.numpy as jnp
from jax import lax
from jax.experimental import pallas as pl
from jax.experimental.pallas import tpu as pltpu
from jax.sharding import PartitionSpec as P

EPSILON = 1e-06
BOTH = ("expert", "tensor")
SIDE = 4
CHIPS = 16
THIRDS = ((0, 336), (336, 688), (688, 1024))
F32 = jnp.float32
BF16 = jnp.bfloat16


def expert_of(y, x, core):
    return (y * SIDE + x) * 2 + core


def masks_of(core):
    return (1, 3) if core == 0 else (3, 1)


def swap_core(value):
    pairs = [(e, e ^ 1) for e in range(2 * CHIPS)]
    return lax.ppermute(value, "expert", pairs)


def shift_z(value, amount):
    pairs = [(z, (z + amount) % SIDE) for z in range(SIDE)]
    return lax.ppermute(value, "tensor", pairs)


def exchange(value, axis, turn):
    pairs = []
    for y in range(SIDE):
        for x in range(SIDE):
            for core in range(2):
                mask = masks_of(core)[turn]
                here = expert_of(y, x, core)
                if axis == "x":
                    pairs.append((here, expert_of(y, x ^ mask, core)))
                elif axis == "y":
                    pairs.append((here, expert_of(y ^ mask, x, core)))
                else:
                    for z in range(SIDE):
                        pairs.append((here * SIDE + z, here * SIDE + (z ^ mask)))
    return lax.ppermute(value, BOTH if axis == "z" else "expert", pairs)


def grow(value, axis, turn):
    return jnp.concatenate([value, exchange(value, axis, turn)], axis=0)


def attend_kernel(length_ref, q_ref, qr_ref, latent_ref, rope_ref, fresh_ref, fresh_rope_ref, out_ref, *, scale, heads):
    request = pl.program_id(0)
    query = q_ref[0]
    query_rope = qr_ref[0]
    latent = latent_ref[0]
    last = (((1,), (1,)), ((), ()))
    scores = lax.dot_general(query, latent, last, preferred_element_type=F32)
    scores = scores + jnp.dot(query_rope, rope_ref[0], preferred_element_type=F32)
    lane = lax.broadcasted_iota(jnp.int32, (1, scores.shape[1]), 1)
    scores = jnp.where(lane < length_ref[request], scores * scale, -1e30)
    fresh = fresh_ref[0]
    fresh_rope = fresh_rope_ref[0]
    recent = lax.dot_general(query, fresh, last, preferred_element_type=F32)
    recent = recent + lax.dot_general(query_rope, fresh_rope, last, preferred_element_type=F32)
    step = lax.broadcasted_iota(jnp.int32, recent.shape, 0) // heads
    place = lax.broadcasted_iota(jnp.int32, recent.shape, 1)
    recent = jnp.where(place <= step, recent * scale, -1e30)
    top = jnp.maximum(
        jnp.max(scores, axis=1, keepdims=True), jnp.max(recent, axis=1, keepdims=True)
    )
    weights = jnp.exp(scores - top)
    recent = jnp.exp(recent - top)
    total = jnp.sum(weights, axis=1, keepdims=True) + jnp.sum(recent, axis=1, keepdims=True)
    share = 1.0 / total
    mixed = jnp.dot((weights * share).astype(BF16), latent, preferred_element_type=F32)
    recent = (recent * share).astype(BF16).astype(F32)
    for n in range(fresh.shape[0]):
        mixed = mixed + recent[:, n : n + 1] * fresh[n : n + 1].astype(F32)
    out_ref[0] = mixed.astype(BF16)


def attention_heads(
    query_latent, query_rope, cache_latent, cache_rope, new_latent, new_rope, lengths, value_proj
):
    requests, steps, heads, latent = query_latent.shape
    rope = query_rope.shape[3]
    context = cache_latent.shape[1]
    rows = steps * heads
    scale = (value_proj.shape[2] + rope) ** (-0.5)
    whole = lambda *shape: pl.BlockSpec((1,) + shape, lambda i, s: (i, 0, 0))
    mixed = pl.pallas_call(
        functools.partial(attend_kernel, scale=scale, heads=heads),
        grid_spec=pltpu.PrefetchScalarGridSpec(
            num_scalar_prefetch=1,
            grid=(requests,),
            in_specs=[
                whole(rows, latent),
                whole(rows, rope),
                whole(context, latent),
                whole(rope, context),
                whole(steps, latent),
                whole(steps, rope),
            ],
            out_specs=whole(rows, latent),
        ),
        out_shape=jax.ShapeDtypeStruct((requests, rows, latent), BF16),
        cost_estimate=pl.CostEstimate(
            flops=2 * requests * rows * context * (2 * latent + rope),
            bytes_accessed=2 * requests * context * (latent + rope),
            transcendentals=requests * rows * context,
        ),
        compiler_params=pltpu.CompilerParams(vmem_limit_bytes=56 << 20),
    )(
        lengths,
        query_latent.reshape(requests, rows, latent),
        query_rope.reshape(requests, rows, rope),
        cache_latent,
        cache_rope,
        new_latent,
        new_rope,
    )
    head_values = jnp.einsum(
        "rshl,hlv->rshv",
        mixed.reshape(requests, steps, heads, latent),
        value_proj,
        preferred_element_type=F32,
    )
    return head_values.astype(BF16).reshape(requests * steps, -1)


def pack_kernel(heads_ref, residual_ref, routing_ref, out_ref, tail, done):
    width = heads_ref.shape[1]
    cols = residual_ref.shape[1] // CHIPS
    copies = [
        pltpu.make_async_copy(heads_ref, out_ref.at[chip, :, pl.ds(0, width)], done.at[chip])
        for chip in range(CHIPS)
    ]
    for copy in copies:
        copy.start()
    for chip in range(CHIPS):
        part = residual_ref[:, chip * cols : (chip + 1) * cols]
        tail[chip] = jnp.concatenate([part, routing_ref[chip]], axis=1)
    last = pltpu.make_async_copy(
        tail, out_ref.at[:, :, pl.ds(width, tail.shape[2])], done.at[CHIPS]
    )
    last.start()
    for copy in copies + [last]:
        copy.wait()


def pack(heads, residual, routing):
    rows, width = heads.shape
    cols = residual.shape[1] // CHIPS
    routing = jnp.pad(routing, ((0, 0), (0, 0), (0, 512 - cols - routing.shape[2])))
    return pl.pallas_call(
        pack_kernel,
        in_specs=[pl.BlockSpec(memory_space=pltpu.VMEM)] * 3,
        out_specs=pl.BlockSpec(memory_space=pl.ANY),
        scratch_shapes=[
            pltpu.VMEM((CHIPS, rows, 512), BF16),
            pltpu.SemaphoreType.DMA((CHIPS + 1,)),
        ],
        out_shape=jax.ShapeDtypeStruct((CHIPS, rows, width + 512), BF16),
        cost_estimate=pl.CostEstimate(
            flops=0, bytes_accessed=2 * CHIPS * rows * (width + 512), transcendentals=0
        ),
    )(heads, residual, routing)


def project_kernel(
    place_ref, in_ref, own_ref, other_ref, gain_ref, out_ref, sum_own, sum_other, *, width
):
    step = pl.program_id(0)
    depth = own_ref.shape[0]

    @pl.when(step == 0)
    def _():
        sum_own[...] = jnp.zeros_like(sum_own)
        sum_other[...] = jnp.zeros_like(sum_other)

    heads = in_ref[:, pl.ds(pl.multiple_of(step * depth, 128), depth)]
    sum_own[...] += jnp.dot(heads, own_ref[...], preferred_element_type=F32)
    sum_other[...] += jnp.dot(heads, other_ref[...], preferred_element_type=F32)

    @pl.when(step == pl.num_programs(0) - 1)
    def _():
        first = place_ref[0] == 0
        own, other = sum_own[...], sum_other[...]
        left = jnp.where(first, own, other)
        right = jnp.where(first, other, own)
        both = jnp.concatenate([left, right], axis=1).astype(BF16).astype(F32)
        tail = in_ref[:, width:].astype(F32)
        cols = both.shape[1]
        stream = tail[:, :cols] + both
        square = jnp.sum(stream * stream, axis=1, keepdims=True)
        high = square.astype(BF16).astype(F32)
        low = square - high
        extra = tail[:, cols:]
        lane = lax.broadcasted_iota(jnp.int32, extra.shape, 1)
        extra = jnp.where(lane == 6, high, jnp.where(lane == 7, low, extra))
        stream = stream * gain_ref[0].astype(F32)
        out_ref[...] = jnp.concatenate([stream, extra], axis=1).astype(BF16)


def project(place, landed, own, other, gain):
    rows, total = landed.shape
    width, cols = own.shape
    steps = 4
    depth = width // steps
    out = total - width
    return pl.pallas_call(
        functools.partial(project_kernel, width=width),
        grid_spec=pltpu.PrefetchScalarGridSpec(
            num_scalar_prefetch=1,
            grid=(steps,),
            in_specs=[
                pl.BlockSpec((rows, total), lambda i, s: (0, 0)),
                pl.BlockSpec((depth, cols), lambda i, s: (i, 0)),
                pl.BlockSpec((depth, cols), lambda i, s: (i, 0)),
                pl.BlockSpec((1, 1, 2 * cols), lambda i, s: (s[1], 0, 0)),
            ],
            out_specs=pl.BlockSpec((rows, out), lambda i, s: (0, 0)),
            scratch_shapes=[pltpu.VMEM((rows, cols), F32)] * 2,
        ),
        out_shape=jax.ShapeDtypeStruct((rows, out), BF16),
        cost_estimate=pl.CostEstimate(
            flops=4 * rows * width * cols, bytes_accessed=4 * width * cols, transcendentals=0
        ),
        compiler_params=pltpu.CompilerParams(vmem_limit_bytes=24 << 20),
    )(place, landed, own, other, gain.reshape(CHIPS, 1, 2 * cols))


def gather_kernel(place_ref, *refs, units, first, final, model):
    counts = [len(rows) for rows, _, _ in units]
    blocks, refs = refs[: sum(counts)], refs[sum(counts) :]
    sources, refs = refs[:4], refs[4:]
    if not first:
        (total_in, own_in), refs = refs[:2], refs[2:]
    if final:
        hidden_ref, index_ref, own_ref, total, tokens, weight, arrived = refs
    else:
        total, own_ref, tokens, weight, arrived = refs
    part = sources[0].shape[1]
    cols = model // CHIPS
    wide = blocks[0].shape[1]
    width = 4 * part
    spare = wide - cols

    def fetch(unit, near):
        chip = place_ref[units[unit][1] * 4 + near]
        source = pl.ds(pl.multiple_of(chip * cols, 64), cols)
        return [
            pltpu.make_async_copy(
                ref.at[source],
                weight.at[unit, pl.ds(near * wide, cols), pl.ds(i * part, part)],
                arrived.at[unit, near, i],
            )
            for i, ref in enumerate(sources)
        ]

    for unit in range(len(units)):
        for near in range(4):
            for copy in fetch(unit, near):
                copy.start()
    for unit in range(len(units)):
        for near in range(4):
            weight[unit, near * wide + cols : (near + 1) * wide] = jnp.zeros((spare, width), BF16)
    if first:
        total[...] = jnp.zeros_like(total)
        own_ref[...] = jnp.zeros_like(own_ref)
    else:
        total[...] = total_in[...]
        own_ref[...] = own_in[...]

    chip = place_ref[20]
    start = pl.multiple_of((chip // 2) * 16, 16)
    for unit, (rows, far, far_z) in enumerate(units):
        here, blocks = blocks[: len(rows)], blocks[len(rows) :]
        for (low, high), ref in zip(rows, here):
            row = low
            while row < high:
                count = min(128 - row % 128, high - row)
                near_z, near = divmod(row // 128, 4)
                at = near_z * 128 + row % 128
                tokens[at : at + count, near * wide : (near + 1) * wide] = ref[
                    row - low : row - low + count
                ]
                row += count
        extra = None
        for near in range(4):
            term = tokens[:, near * wide + cols : (near + 1) * wide].astype(F32)
            extra = term if extra is None else extra + term
            if far == 0 and near == 0:
                total[far_z, :, width + spare :] = term
            if far_z == 0:
                mine = tokens[pl.ds(start, 16), near * wide : (near + 1) * wide].astype(F32)
                own_ref[pl.ds(place_ref[far * 4 + near], 1)] = jnp.where(
                    lax.rem(chip, 2) == 0, mine[:8], mine[8:]
                )[None]
            for copy in fetch(unit, near):
                copy.wait()
        total[far_z, :, width : width + spare] += extra
        total[far_z, :, :width] += jnp.dot(
            tokens[...], weight[unit], preferred_element_type=F32
        )
    if not final:
        return

    group = lax.broadcasted_iota(jnp.int32, (128, 1), 0) // 8
    half = total.shape[1]
    slots = 4 * 4 * CHIPS
    lanes = lax.broadcasted_iota(jnp.int32, (1, slots), 1)
    even = place_ref[21] == 0
    sums = [None, None]
    for far_z in range(2):
        extra = total[far_z, :, width:]
        square = (extra[:, 6:7] + extra[:, 7:8]) * (1.0 / model)
        inverse = lax.rsqrt(square + EPSILON)
        names = extra[:, spare:]
        bases = jnp.concatenate(
            [group * 4 + place_ref[16 + far_z * 2 + i] * (4 * CHIPS) for i in range(2)], axis=0
        )
        gates = [names[:, 2 * i : 2 * i + 1] + names[:, 2 * i + 1 : 2 * i + 2] for i in range(2)]
        ranks = [names[:, 4 + i : 5 + i].astype(jnp.int32) for i in range(2)]
        for i in range(2):
            gate = total[far_z, :, i * part : (i + 1) * part] * inverse
            up = total[far_z, :, (2 + i) * part : (3 + i) * part] * inverse
            share = jnp.where(even, gates[i], gates[1 - i])
            rank = jnp.where(even, ranks[i], ranks[1 - i])
            value = gate * (1.0 / (1.0 + jnp.exp(-gate))) * up * share
            place_index = jnp.where(rank < 4, bases + rank, -1)
            index_ref[far_z * half : (far_z + 1) * half, i : i + 1] = place_index
            hot = (place_index == lanes).astype(BF16)
            term = lax.dot_general(
                hot, value.astype(BF16), (((0,), (0,)), ((), ())), preferred_element_type=F32
            )
            sums[i] = term if sums[i] is None else sums[i] + term
    for i in range(2):
        hidden_ref[i] = sums[i].astype(BF16)


def gather_products(place, units, blocks, weights, carried, final):
    model, part = weights[0].shape
    wide = blocks[0].shape[1]
    width = 4 * part
    tok = SIDE * 128
    spare = wide - model // CHIPS
    whole = lambda *shape: pl.BlockSpec(shape, lambda i, s: (0,) * len(shape))
    total_shape = (2, tok // 2, width + 2 * spare)
    own_shape = (CHIPS, 8, wide)
    scratch = [
        pltpu.VMEM((tok // 2, 4 * wide), BF16),
        pltpu.VMEM((len(units), 4 * wide, width), BF16),
        pltpu.SemaphoreType.DMA((len(units), 4, 4)),
    ]
    if final:
        outs = [((2, tok // 2, part), BF16), ((tok, 2), jnp.int32), (own_shape, F32)]
        scratch = [pltpu.VMEM(total_shape, F32)] + scratch
    else:
        outs = [(total_shape, F32), (own_shape, F32)]
    return pl.pallas_call(
        functools.partial(
            gather_kernel, units=units, first=carried is None, final=final, model=model
        ),
        grid_spec=pltpu.PrefetchScalarGridSpec(
            num_scalar_prefetch=1,
            grid=(1,),
            in_specs=[whole(*b.shape) for b in blocks]
            + [pl.BlockSpec(memory_space=pltpu.HBM)] * 4
            + ([] if carried is None else [whole(*total_shape), whole(*own_shape)]),
            out_specs=[whole(*shape) for shape, _ in outs],
            scratch_shapes=scratch,
        ),
        out_shape=[jax.ShapeDtypeStruct(shape, kind) for shape, kind in outs],
        cost_estimate=pl.CostEstimate(
            flops=len(units) * tok * 4 * wide * width,
            bytes_accessed=len(units) * 8 * wide * width,
            transcendentals=0,
        ),
        compiler_params=pltpu.CompilerParams(vmem_limit_bytes=44 << 20),
    )(place, *blocks, *weights, *(() if carried is None else carried))


def down_kernel(place_ref, index_ref, *refs):
    hidden, weights, (out_ref, spread) = refs[:4], refs[4:12], refs[12:]
    slots, part = hidden[0].shape[1:]

    @pl.when(pl.program_id(0) == 0)
    def _():
        lanes = lax.broadcasted_iota(jnp.int32, (1, slots), 1)
        for i in range(2):
            hot = (index_ref[:, i : i + 1] == lanes).astype(BF16)
            for k, ref in enumerate(hidden):
                at = (i * 4 + (k if i == 0 else (0, 2, 1, 3)[k])) * part
                spread[:, at : at + part] = jnp.dot(
                    hot, ref[i], preferred_element_type=F32
                ).astype(BF16)

    weight = jnp.concatenate([ref[...] for ref in weights], axis=0)
    total = jnp.dot(spread[...], weight, preferred_element_type=F32).astype(BF16)
    for i in range(4):
        start = pl.multiple_of(place_ref[16 + i] * 128, 128)
        out_ref[pl.ds(start, 128), :] = total[i * 128 : (i + 1) * 128]


def down(place, index, hidden, own, other):
    tok = index.shape[0]
    slots, part = hidden[0].shape[1:]
    width = own[1].shape[1]
    tile = width // 2
    h_spec = pl.BlockSpec((2, slots, part), lambda i, s: (0, 0, 0))
    return pl.pallas_call(
        down_kernel,
        grid_spec=pltpu.PrefetchScalarGridSpec(
            num_scalar_prefetch=1,
            grid=(width // tile,),
            in_specs=[pl.BlockSpec((tok, 2), lambda i, s: (0, 0))]
            + [h_spec] * 4
            + [pl.BlockSpec((part, tile), lambda i, s: (0, s[22] * 2 + i))]
            + [pl.BlockSpec((part, tile), lambda i, s: (0, i))] * 7,
            out_specs=pl.BlockSpec((tok, tile), lambda i, s: (0, i)),
            scratch_shapes=[pltpu.VMEM((tok, 8 * part), BF16)],
        ),
        out_shape=jax.ShapeDtypeStruct((tok, width), BF16),
        cost_estimate=pl.CostEstimate(
            flops=16 * tok * part * width, bytes_accessed=16 * part * width, transcendentals=0
        ),
        compiler_params=pltpu.CompilerParams(vmem_limit_bytes=48 << 20),
    )(place, index, *hidden, *own, *other)


def routing_columns(expert_ids, expert_gates):
    rows, count = expert_ids.shape
    experts = 2 * CHIPS
    hot = expert_ids[:, :, None] == jnp.arange(experts, dtype=jnp.int32)
    gates = jnp.sum(jnp.where(hot, expert_gates[:, :, None], 0.0), axis=1)
    named = jnp.any(hot, axis=1)
    ones = named.astype(F32)
    below = jnp.tril(jnp.ones((rows, rows), F32), -1)
    rank = jnp.where(named, jnp.sum(below[:, :, None] * ones[None], axis=1), 8.0)
    high = lax.reduce_precision(gates, 8, 7)
    low = gates - high
    pair = lambda v: v.reshape(rows, CHIPS, 2).transpose(1, 0, 2)
    gate_pair = jnp.stack([pair(high), pair(low)], axis=-1).reshape(CHIPS, rows, 4)
    return jnp.concatenate([gate_pair, pair(rank)], axis=-1).astype(BF16)


def per_device(
    residual,
    query_latent,
    query_rope,
    cache_latent,
    cache_rope,
    new_latent,
    new_rope,
    lengths,
    value_proj,
    out_proj,
    norm_gain,
    expert_ids,
    expert_gates,
    w_gate,
    w_up,
    w_down,
):
    rows, model = residual.shape
    expert = lax.axis_index("expert")
    plane = lax.axis_index("tensor")
    core = expert % 2
    chip = expert // 2
    first = jnp.where(core == 0, 1, 3)
    second = 4 - first
    table = []
    for far_y in range(2):
        for far_x in range(2):
            for near_y in range(2):
                for near_x in range(2):
                    mask_x = (first * near_x) ^ (second * far_x)
                    mask_y = (first * near_y) ^ (second * far_y)
                    table.append(chip ^ (mask_y * SIDE + mask_x))
    for far_z in range(2):
        for near_z in range(2):
            table.append(plane ^ ((first * near_z) ^ (second * far_z)))
    table += [chip, core, plane, chip]
    place = jnp.stack([jnp.asarray(v, jnp.int32) for v in table])

    quarter = model // SIDE
    half = w_down.shape[1]
    cut = lambda v, z: lax.dynamic_slice(v, (0, z * quarter), (half, quarter))
    lengths, passed, near = lax.optimization_barrier(
        (lengths, cut(w_down[0], plane ^ first ^ second), cut(w_down[0], plane ^ first))
    )
    passed, near = exchange(passed, "z", 0), exchange(near, "z", 0)
    out_other = swap_core(out_proj.T)
    gate_own, up_own = w_gate[0], w_up[0]
    gate_other, up_other = swap_core(gate_own), swap_core(up_own)

    heads = attention_heads(
        query_latent,
        query_rope,
        cache_latent,
        cache_rope,
        new_latent,
        new_rope,
        lengths,
        value_proj,
    )
    cols = model // CHIPS
    sent = pack(heads, residual, routing_columns(expert_ids, expert_gates))
    sent, out_other, gate_other, up_other, passed, late_down = lax.optimization_barrier(
        (sent, out_other, gate_other, up_other, passed, w_down[0])
    )
    far = exchange(cut(late_down, plane ^ second), "z", 1)
    lane_plane = [
        [expert_of(y, x, core) for y in range(SIDE) for x in range(SIDE)] for core in range(2)
    ]
    landed = lax.all_to_all(
        sent, "expert", split_axis=0, concat_axis=0, tiled=True, axis_index_groups=lane_plane
    )
    landed, near, far = lax.optimization_barrier((landed, near, far))
    block = project(
        jnp.stack([core, chip]).astype(jnp.int32),
        landed.reshape(CHIPS * rows, -1),
        out_proj,
        out_other.T,
        norm_gain,
    )
    last = exchange(passed, "z", 1)
    block = grow(block, "x", 0)
    block = grow(block, "y", 0)
    block, last = lax.optimization_barrier((block, last))
    block = grow(block, "z", 0)
    others = [swap_core(v) for v in (cut(late_down, plane), near, far, last)]
    weights = (gate_own, gate_other, up_own, up_other)
    all_rows = (THIRDS[0][:1] + THIRDS[-1][1:],)
    by_x, by_y, by_z = exchange(block, "x", 1), exchange(block, "y", 1), exchange(block, "z", 1)
    carried = gather_products(place, ((all_rows, 0, 0),), (block,), weights, None, False)
    own, on_x = lax.optimization_barrier((carried[1], by_x))
    own, on_y = lax.optimization_barrier((own, by_y))
    own, on_z, *others[:2] = lax.optimization_barrier((own, by_z, *others[:2]))
    carried = (carried[0], own)
    by_xy, by_yz, by_xz = exchange(on_x, "y", 1), exchange(on_y, "z", 1), exchange(on_z, "x", 1)
    carried = gather_products(
        place,
        ((all_rows, 1, 0), (all_rows, 2, 0), (all_rows, 0, 1)),
        (by_x, by_y, by_z),
        weights,
        carried,
        False,
    )
    cuts = [
        value[low:high] for value, (low, high) in zip((by_xy, by_yz, by_xz), THIRDS)
    ]
    own, cuts[0] = lax.optimization_barrier((carried[1], cuts[0]))
    own, cuts[1] = lax.optimization_barrier((own, cuts[1]))
    own, cuts[2], others[2], others[3] = lax.optimization_barrier(
        (own, cuts[2], others[2], others[3])
    )
    carried = (carried[0], own)
    thirds = [exchange(value, axis, 1) for value, axis in zip(cuts, "zxy")]
    carried = gather_products(
        place,
        ((all_rows, 3, 0), (all_rows, 2, 1), (all_rows, 1, 1)),
        (by_xy, by_yz, by_xz),
        weights,
        carried,
        False,
    )
    hidden, index, own = gather_products(
        place, ((THIRDS, 3, 1),), tuple(thirds), weights, carried, True
    )
    spread = [hidden, exchange(hidden, "z", 0), exchange(hidden, "z", 1), shift_z(hidden, 2)]
    sums = down(place, index, spread, (w_down[0], near, far, last), others)
    lane_all = [
        [expert_of(y, x, core) * SIDE + z for z in range(SIDE) for y in range(SIDE) for x in range(SIDE)]
        for core in range(2)
    ]
    returned = lax.all_to_all(
        sums.reshape(SIDE * CHIPS, rows, quarter),
        BOTH,
        split_axis=0,
        concat_axis=0,
        tiled=True,
        axis_index_groups=lane_all,
    )
    routed = jnp.sum(returned.reshape(SIDE, CHIPS, rows, quarter).astype(F32), axis=1)
    routed = routed.transpose(1, 0, 2).reshape(rows, model)
    stream = own[:, :, :cols].transpose(1, 0, 2).reshape(rows, model) / norm_gain.astype(F32)
    return (stream + routed).astype(BF16)


def solution(mesh):
    return jax.shard_map(
        per_device,
        mesh=mesh,
        in_specs=(
            P(BOTH, None),
            P(BOTH, None, None, None),
            P(BOTH, None, None, None),
            P(BOTH, None, None),
            P(BOTH, None, None),
            P(BOTH, None, None),
            P(BOTH, None, None),
            P(BOTH),
            P(),
            P(None, "expert"),
            P(),
            P(BOTH, None),
            P(BOTH, None),
            P("expert", None, "tensor"),
            P("expert", None, "tensor"),
            P("expert", "tensor", None),
        ),
        out_specs=P(BOTH, None),
        check_vma=False,
    )
```

```python
import functools

import jax
import jax.numpy as jnp
from jax import lax
from jax.experimental import pallas as pl
from jax.experimental.pallas import tpu as pltpu
from jax.sharding import PartitionSpec as P

EPSILON = 1e-06
BOTH = ("expert", "tensor")
SIDE = 4
CHIPS = 16
HALVES = ((0, 512), (512, 1024))
F32 = jnp.float32
BF16 = jnp.bfloat16


def expert_of(y, x, core):
    return (y * SIDE + x) * 2 + core


def masks_of(core):
    return (1, 3) if core == 0 else (3, 1)


def swap_core(value):
    pairs = [(e, e ^ 1) for e in range(2 * CHIPS)]
    return lax.ppermute(value, "expert", pairs)


def shift_z(value, amount):
    pairs = [(z, (z + amount) % SIDE) for z in range(SIDE)]
    return lax.ppermute(value, "tensor", pairs)


def exchange(value, axis, turn):
    pairs = []
    for y in range(SIDE):
        for x in range(SIDE):
            for core in range(2):
                mask = masks_of(core)[turn]
                here = expert_of(y, x, core)
                if axis == "x":
                    pairs.append((here, expert_of(y, x ^ mask, core)))
                elif axis == "y":
                    pairs.append((here, expert_of(y ^ mask, x, core)))
                else:
                    for z in range(SIDE):
                        pairs.append((here * SIDE + z, here * SIDE + (z ^ mask)))
    return lax.ppermute(value, BOTH if axis == "z" else "expert", pairs)


def pairs_of(core):
    mask = masks_of(core)[0]
    return [(v, v ^ mask) for v in range(SIDE) if v < v ^ mask]


def attend_kernel(length_ref, q_ref, qr_ref, latent_ref, rope_ref, fresh_ref, fresh_rope_ref, out_ref, *, scale, heads):
    request = pl.program_id(0)
    query = q_ref[0]
    query_rope = qr_ref[0]
    latent = latent_ref[0]
    last = (((1,), (1,)), ((), ()))
    scores = lax.dot_general(query, latent, last, preferred_element_type=F32)
    scores = scores + jnp.dot(query_rope, rope_ref[0], preferred_element_type=F32)
    lane = lax.broadcasted_iota(jnp.int32, (1, scores.shape[1]), 1)
    scores = jnp.where(lane < length_ref[request], scores * scale, -1e30)
    fresh = fresh_ref[0]
    fresh_rope = fresh_rope_ref[0]
    recent = lax.dot_general(query, fresh, last, preferred_element_type=F32)
    recent = recent + lax.dot_general(query_rope, fresh_rope, last, preferred_element_type=F32)
    step = lax.broadcasted_iota(jnp.int32, recent.shape, 0) // heads
    place = lax.broadcasted_iota(jnp.int32, recent.shape, 1)
    recent = jnp.where(place <= step, recent * scale, -1e30)
    top = jnp.maximum(
        jnp.max(scores, axis=1, keepdims=True), jnp.max(recent, axis=1, keepdims=True)
    )
    weights = jnp.exp(scores - top)
    recent = jnp.exp(recent - top)
    total = jnp.sum(weights, axis=1, keepdims=True) + jnp.sum(recent, axis=1, keepdims=True)
    share = 1.0 / total
    mixed = jnp.dot((weights * share).astype(BF16), latent, preferred_element_type=F32)
    recent = (recent * share).astype(BF16).astype(F32)
    for n in range(fresh.shape[0]):
        mixed = mixed + recent[:, n : n + 1] * fresh[n : n + 1].astype(F32)
    out_ref[0] = mixed.astype(BF16)


def attention_heads(
    query_latent, query_rope, cache_latent, cache_rope, new_latent, new_rope, lengths, value_proj
):
    requests, steps, heads, latent = query_latent.shape
    rope = query_rope.shape[3]
    context = cache_latent.shape[1]
    rows = steps * heads
    scale = (value_proj.shape[2] + rope) ** (-0.5)
    whole = lambda *shape: pl.BlockSpec((1,) + shape, lambda i, s: (i, 0, 0))
    mixed = pl.pallas_call(
        functools.partial(attend_kernel, scale=scale, heads=heads),
        grid_spec=pltpu.PrefetchScalarGridSpec(
            num_scalar_prefetch=1,
            grid=(requests,),
            in_specs=[
                whole(rows, latent),
                whole(rows, rope),
                whole(context, latent),
                whole(rope, context),
                whole(steps, latent),
                whole(steps, rope),
            ],
            out_specs=whole(rows, latent),
        ),
        out_shape=jax.ShapeDtypeStruct((requests, rows, latent), BF16),
        cost_estimate=pl.CostEstimate(
            flops=2 * requests * rows * context * (2 * latent + rope),
            bytes_accessed=2 * requests * context * (latent + rope),
            transcendentals=requests * rows * context,
        ),
        compiler_params=pltpu.CompilerParams(vmem_limit_bytes=56 << 20),
    )(
        lengths,
        query_latent.reshape(requests, rows, latent),
        query_rope.reshape(requests, rows, rope),
        cache_latent,
        cache_rope,
        new_latent,
        new_rope,
    )
    head_values = jnp.einsum(
        "rshl,hlv->hrsv",
        mixed.reshape(requests, steps, heads, latent),
        value_proj,
        preferred_element_type=F32,
    )
    return head_values.astype(BF16).reshape(heads, requests * steps, -1)


def pack_kernel(
    heads_ref, residual_ref, ids_ref, gates_ref, out_ref, values, tail, done
):
    heads, rows, each = heads_ref.shape
    width = heads * each
    cols = residual_ref.shape[1] // CHIPS
    for head in range(heads):
        values[:, head * each : (head + 1) * each] = heads_ref[head]
    copies = [
        pltpu.make_async_copy(values, out_ref.at[chip, :, pl.ds(0, width)], done.at[chip])
        for chip in range(CHIPS)
    ]
    for copy in copies:
        copy.start()
    lane = lax.broadcasted_iota(jnp.int32, (rows, 128), 1)
    gates = jnp.zeros((rows, 128), F32)
    named = jnp.zeros((rows, 128), F32)
    for k in range(ids_ref.shape[1]):
        match = ids_ref[:, k : k + 1] == lane
        gates = gates + jnp.where(match, gates_ref[:, k : k + 1], 0.0)
        named = named + jnp.where(match, 1.0, 0.0)
    above = lax.broadcasted_iota(jnp.int32, (rows, rows), 1)
    below = above < lax.broadcasted_iota(jnp.int32, (rows, rows), 0)
    below = jnp.where(below, 1.0, 0.0).astype(BF16)
    rank = jnp.dot(below, named.astype(BF16), preferred_element_type=F32)
    rank = jnp.where(named > 0.5, rank, 8.0)
    high = gates.astype(BF16).astype(F32)
    low = gates - high
    for chip in range(CHIPS):
        at = 128 - 2 * chip
        picked = jnp.where(
            lane < 2,
            pltpu.roll(high, at % 128, 1),
            jnp.where(
                lane < 4, pltpu.roll(low, (at + 2) % 128, 1), pltpu.roll(rank, (at + 4) % 128, 1)
            ),
        )
        picked = jnp.where(lane < 6, picked, 0.0)[:, : 512 - cols]
        part = residual_ref[:, chip * cols : (chip + 1) * cols]
        tail[chip] = jnp.concatenate([part, picked.astype(BF16)], axis=1)
    last = pltpu.make_async_copy(
        tail, out_ref.at[:, :, pl.ds(width, tail.shape[2])], done.at[CHIPS]
    )
    last.start()
    for copy in copies + [last]:
        copy.wait()


def pack(heads, residual, ids, gates):
    count, rows, each = heads.shape
    width = count * each
    return pl.pallas_call(
        pack_kernel,
        in_specs=[pl.BlockSpec(memory_space=pltpu.VMEM)] * 4,
        out_specs=pl.BlockSpec(memory_space=pl.ANY),
        scratch_shapes=[
            pltpu.VMEM((rows, width), BF16),
            pltpu.VMEM((CHIPS, rows, 512), BF16),
            pltpu.SemaphoreType.DMA((CHIPS + 1,)),
        ],
        out_shape=jax.ShapeDtypeStruct((CHIPS, rows, width + 512), BF16),
        cost_estimate=pl.CostEstimate(
            flops=0, bytes_accessed=2 * CHIPS * rows * (width + 512), transcendentals=0
        ),
    )(heads, residual, ids, gates)


def project_kernel(
    place_ref, in_ref, own_ref, other_ref, gain_ref, out_ref, sum_own, sum_other, *, width
):
    step = pl.program_id(0)
    depth = own_ref.shape[0]

    @pl.when(step == 0)
    def _():
        sum_own[...] = jnp.zeros_like(sum_own)
        sum_other[...] = jnp.zeros_like(sum_other)

    heads = in_ref[:, pl.ds(pl.multiple_of(step * depth, 128), depth)]
    sum_own[...] += jnp.dot(heads, own_ref[...], preferred_element_type=F32)
    sum_other[...] += jnp.dot(heads, other_ref[...], preferred_element_type=F32)

    @pl.when(step == pl.num_programs(0) - 1)
    def _():
        first = place_ref[0] == 0
        own, other = sum_own[...], sum_other[...]
        left = jnp.where(first, own, other)
        right = jnp.where(first, other, own)
        both = jnp.concatenate([left, right], axis=1).astype(BF16).astype(F32)
        tail = in_ref[:, width:].astype(F32)
        cols = both.shape[1]
        stream = tail[:, :cols] + both
        square = jnp.sum(stream * stream, axis=1, keepdims=True)
        high = square.astype(BF16).astype(F32)
        low = square - high
        extra = tail[:, cols:]
        lane = lax.broadcasted_iota(jnp.int32, extra.shape, 1)
        extra = jnp.where(lane == 6, high, jnp.where(lane == 7, low, extra))
        stream = stream * gain_ref[0].astype(F32)
        value = jnp.concatenate([stream, extra], axis=1).astype(BF16)
        for i in range(out_ref.shape[0]):
            out_ref[i] = value


def project(place, landed, own, other, gain):
    rows, total = landed.shape
    width, cols = own.shape
    steps = 4
    depth = width // steps
    out = total - width
    return pl.pallas_call(
        functools.partial(project_kernel, width=width),
        grid_spec=pltpu.PrefetchScalarGridSpec(
            num_scalar_prefetch=1,
            grid=(steps,),
            in_specs=[
                pl.BlockSpec((rows, total), lambda i, s: (0, 0)),
                pl.BlockSpec((depth, cols), lambda i, s: (i, 0)),
                pl.BlockSpec((depth, cols), lambda i, s: (i, 0)),
                pl.BlockSpec((1, 1, 2 * cols), lambda i, s: (s[1], 0, 0)),
            ],
            out_specs=pl.BlockSpec((8, rows, out), lambda i, s: (0, 0, 0)),
            scratch_shapes=[pltpu.VMEM((rows, cols), F32)] * 2,
        ),
        out_shape=jax.ShapeDtypeStruct((8, rows, out), BF16),
        cost_estimate=pl.CostEstimate(
            flops=4 * rows * width * cols, bytes_accessed=4 * width * cols, transcendentals=0
        ),
        compiler_params=pltpu.CompilerParams(vmem_limit_bytes=24 << 20),
    )(place, landed, own, other, gain.reshape(CHIPS, 1, 2 * cols))


def gather_kernel(place_ref, *refs, units, first, final, model):
    counts = [len(rows) for rows, _, _ in units]
    blocks, refs = refs[: sum(counts)], refs[sum(counts) :]
    sources, refs = refs[:4], refs[4:]
    if not first:
        (total_in, own_in), refs = refs[:2], refs[2:]
    if final:
        hidden_ref, index_ref, own_ref, total, tokens, weight, arrived = refs
    else:
        total, own_ref, tokens, weight, arrived = refs
    part = sources[0].shape[1]
    cols = model // CHIPS
    wide = blocks[0].shape[1]
    width = 4 * part
    spare = wide - cols

    def fetch(unit, near):
        chip = place_ref[units[unit][1] * 4 + near]
        source = pl.ds(pl.multiple_of(chip * cols, 64), cols)
        return [
            pltpu.make_async_copy(
                ref.at[source],
                weight.at[unit, pl.ds(near * wide, cols), pl.ds(i * part, part)],
                arrived.at[unit, near, i],
            )
            for i, ref in enumerate(sources)
        ]

    for unit in range(len(units)):
        for near in range(4):
            for copy in fetch(unit, near):
                copy.start()
    for unit in range(len(units)):
        for near in range(4):
            weight[unit, near * wide + cols : (near + 1) * wide] = jnp.zeros((spare, width), BF16)
    if first:
        total[...] = jnp.zeros_like(total)
        own_ref[...] = jnp.zeros_like(own_ref)
    else:
        total[...] = total_in[...]
        own_ref[...] = own_in[...]

    chip = place_ref[20]
    start = pl.multiple_of(place_ref[24] * 128 + (chip // 2) * 16, 16)
    for unit, (rows, far, far_z) in enumerate(units):
        here, blocks = blocks[: len(rows)], blocks[len(rows) :]
        for (low, high), ref in zip(rows, here):
            row = low
            while row < high:
                count = min(128 - row % 128, high - row)
                near_z, near = divmod(row // 128, 4)
                at = near_z * 128 + row % 128
                tokens[at : at + count, near * wide : (near + 1) * wide] = ref[
                    row - low : row - low + count
                ]
                row += count
        extra = None
        for near in range(4):
            term = tokens[:, near * wide + cols : (near + 1) * wide].astype(F32)
            extra = term if extra is None else extra + term
            if far_z == 0:
                mine = tokens[pl.ds(start, 16), near * wide : (near + 1) * wide].astype(F32)
                own_ref[pl.ds(place_ref[far * 4 + near], 1)] = jnp.where(
                    lax.rem(chip, 2) == 0, mine[:8], mine[8:]
                )[None]
            for copy in fetch(unit, near):
                copy.wait()
        if far == 0:
            at = pl.multiple_of(place_ref[23] * wide + cols // 128 * 128, 128)
            total[far_z, :, width + spare :] = tokens[:, pl.ds(at, 128)][:, cols % 128 :].astype(
                F32
            )
        total[far_z, :, width : width + spare] += extra
        total[far_z, :, :width] += jnp.dot(
            tokens[...], weight[unit], preferred_element_type=F32
        )
    if not final:
        return

    group = lax.broadcasted_iota(jnp.int32, (128, 1), 0) // 8
    half = total.shape[1]
    slots = 4 * 4 * CHIPS
    lanes = lax.broadcasted_iota(jnp.int32, (1, slots), 1)
    even = place_ref[21] == 0
    sums = [None, None]
    for far_z in range(2):
        extra = total[far_z, :, width:]
        square = (extra[:, 6:7] + extra[:, 7:8]) * (1.0 / model)
        inverse = lax.rsqrt(square + EPSILON)
        names = extra[:, spare:]
        bases = jnp.concatenate(
            [group * 4 + place_ref[16 + far_z * 2 + i] * (4 * CHIPS) for i in range(2)], axis=0
        )
        gates = [names[:, i : i + 1] + names[:, 2 + i : 3 + i] for i in range(2)]
        ranks = [names[:, 4 + i : 5 + i].astype(jnp.int32) for i in range(2)]
        for i in range(2):
            gate = total[far_z, :, i * part : (i + 1) * part] * inverse
            up = total[far_z, :, (2 + i) * part : (3 + i) * part] * inverse
            share = jnp.where(even, gates[i], gates[1 - i])
            rank = jnp.where(even, ranks[i], ranks[1 - i])
            value = gate * (1.0 / (1.0 + jnp.exp(-gate))) * up * share
            place_index = jnp.where(rank < 4, bases + rank, -1)
            index_ref[far_z * half : (far_z + 1) * half, i : i + 1] = place_index
            hot = (place_index == lanes).astype(BF16)
            term = lax.dot_general(
                hot, value.astype(BF16), (((0,), (0,)), ((), ())), preferred_element_type=F32
            )
            sums[i] = term if sums[i] is None else sums[i] + term
    for i in range(2):
        hidden_ref[i] = sums[i].astype(BF16)


def gather_products(place, units, blocks, weights, carried, final):
    model, part = weights[0].shape
    wide = blocks[0].shape[1]
    width = 4 * part
    tok = SIDE * 128
    spare = wide - model // CHIPS
    whole = lambda *shape: pl.BlockSpec(shape, lambda i, s: (0,) * len(shape))
    total_shape = (2, tok // 2, width + 2 * spare)
    own_shape = (CHIPS, 8, wide)
    scratch = [
        pltpu.VMEM((tok // 2, 4 * wide), BF16),
        pltpu.VMEM((len(units), 4 * wide, width), BF16),
        pltpu.SemaphoreType.DMA((len(units), 4, 4)),
    ]
    if final:
        outs = [((2, tok // 2, part), BF16), ((tok, 2), jnp.int32), (own_shape, F32)]
        scratch = [pltpu.VMEM(total_shape, F32)] + scratch
    else:
        outs = [(total_shape, F32), (own_shape, F32)]
    return pl.pallas_call(
        functools.partial(
            gather_kernel, units=units, first=carried is None, final=final, model=model
        ),
        grid_spec=pltpu.PrefetchScalarGridSpec(
            num_scalar_prefetch=1,
            grid=(1,),
            in_specs=[whole(*b.shape) for b in blocks]
            + [pl.BlockSpec(memory_space=pltpu.HBM)] * 4
            + ([] if carried is None else [whole(*total_shape), whole(*own_shape)]),
            out_specs=[whole(*shape) for shape, _ in outs],
            scratch_shapes=scratch,
        ),
        out_shape=[jax.ShapeDtypeStruct(shape, kind) for shape, kind in outs],
        cost_estimate=pl.CostEstimate(
            flops=len(units) * tok * 4 * wide * width,
            bytes_accessed=len(units) * 8 * wide * width,
            transcendentals=0,
        ),
        compiler_params=pltpu.CompilerParams(vmem_limit_bytes=44 << 20),
    )(place, *blocks, *weights, *(() if carried is None else carried))


def down_kernel(place_ref, index_ref, *refs):
    hidden, weights, (out_ref, spread) = refs[:4], refs[4:12], refs[12:]
    slots, part = hidden[0].shape[1:]

    @pl.when(pl.program_id(0) == 0)
    def _():
        lanes = lax.broadcasted_iota(jnp.int32, (1, slots), 1)
        for i in range(2):
            hot = (index_ref[:, i : i + 1] == lanes).astype(BF16)
            for k, ref in enumerate(hidden):
                at = (i * 4 + (k if i == 0 else (0, 2, 1, 3)[k])) * part
                spread[:, at : at + part] = jnp.dot(
                    hot, ref[i], preferred_element_type=F32
                ).astype(BF16)

    weight = jnp.concatenate([ref[...] for ref in weights], axis=0)
    total = jnp.dot(spread[...], weight, preferred_element_type=F32).astype(BF16)
    for i in range(4):
        start = pl.multiple_of(place_ref[16 + i] * 128, 128)
        out_ref[pl.ds(start, 128), :] = total[i * 128 : (i + 1) * 128]


def down(place, index, hidden, own, other):
    tok = index.shape[0]
    slots, part = hidden[0].shape[1:]
    width = own[1].shape[1]
    tile = width // 2
    h_spec = pl.BlockSpec((2, slots, part), lambda i, s: (0, 0, 0))
    return pl.pallas_call(
        down_kernel,
        grid_spec=pltpu.PrefetchScalarGridSpec(
            num_scalar_prefetch=1,
            grid=(width // tile,),
            in_specs=[pl.BlockSpec((tok, 2), lambda i, s: (0, 0))]
            + [h_spec] * 4
            + [pl.BlockSpec((part, tile), lambda i, s: (0, s[22] * 2 + i))]
            + [pl.BlockSpec((part, tile), lambda i, s: (0, i))] * 7,
            out_specs=pl.BlockSpec((tok, tile), lambda i, s: (0, i)),
            scratch_shapes=[pltpu.VMEM((tok, 8 * part), BF16)],
        ),
        out_shape=jax.ShapeDtypeStruct((tok, width), BF16),
        cost_estimate=pl.CostEstimate(
            flops=16 * tok * part * width, bytes_accessed=16 * part * width, transcendentals=0
        ),
        compiler_params=pltpu.CompilerParams(vmem_limit_bytes=28 << 20),
    )(place, index, *hidden, *own, *other)


def per_device(
    residual,
    query_latent,
    query_rope,
    cache_latent,
    cache_rope,
    new_latent,
    new_rope,
    lengths,
    value_proj,
    out_proj,
    norm_gain,
    expert_ids,
    expert_gates,
    w_gate,
    w_up,
    w_down,
):
    rows, model = residual.shape
    expert = lax.axis_index("expert")
    plane = lax.axis_index("tensor")
    core = expert % 2
    chip = expert // 2
    first = jnp.where(core == 0, 1, 3)
    second = 4 - first
    pair = lambda v: (jnp.minimum(v, v ^ first), jnp.maximum(v, v ^ first))
    row, column = chip // SIDE, chip % SIDE
    table = []
    for far_y in range(2):
        for far_x in range(2):
            for near_y in range(2):
                for near_x in range(2):
                    table.append(
                        pair(row ^ (second * far_y))[near_y] * SIDE
                        + pair(column ^ (second * far_x))[near_x]
                    )
    for far_z in range(2):
        for near_z in range(2):
            table.append(pair(plane ^ (second * far_z))[near_z])
    is_high = lambda v: jnp.where(v == pair(v)[1], 1, 0)
    table += [chip, core, plane, is_high(row) * 2 + is_high(column), is_high(plane)]
    place = jnp.stack([jnp.asarray(v, jnp.int32) for v in table])

    quarter = model // SIDE
    half = w_down.shape[1]
    cut = lambda v, z: lax.dynamic_slice(v, (0, z * quarter), (half, quarter))
    lengths, passed, near = lax.optimization_barrier(
        (lengths, cut(w_down[0], plane ^ first ^ second), cut(w_down[0], plane ^ first))
    )
    passed, near = exchange(passed, "z", 0), exchange(near, "z", 0)
    out_other = swap_core(out_proj.T)
    gate_own, up_own = w_gate[0], w_up[0]
    gate_other, up_other = swap_core(gate_own), swap_core(up_own)

    heads = attention_heads(
        query_latent,
        query_rope,
        cache_latent,
        cache_rope,
        new_latent,
        new_rope,
        lengths,
        value_proj,
    )
    cols = model // CHIPS
    sent = pack(heads, residual, expert_ids, expert_gates)
    sent, out_other, gate_other, up_other, passed, late_down = lax.optimization_barrier(
        (sent, out_other, gate_other, up_other, passed, w_down[0])
    )
    here = cut(late_down, plane)
    far = exchange(cut(late_down, plane ^ second), "z", 1)
    lane_plane = [
        [expert_of(y, x, core) for y in range(SIDE) for x in range(SIDE)] for core in range(2)
    ]
    landed = lax.all_to_all(
        sent, "expert", split_axis=0, concat_axis=0, tiled=True, axis_index_groups=lane_plane
    )
    landed, near, far = lax.optimization_barrier((landed, near, far))
    block = project(
        jnp.stack([core, chip]).astype(jnp.int32),
        landed.reshape(CHIPS * rows, -1),
        out_proj,
        out_other.T,
        norm_gain,
    )
    last = exchange(passed, "z", 1)
    cubes = [
        [expert_of(y, x, core) * SIDE + z for z in z_pair for y in y_pair for x in x_pair]
        for core in range(2)
        for z_pair in pairs_of(core)
        for y_pair in pairs_of(core)
        for x_pair in pairs_of(core)
    ]
    block = lax.all_to_all(
        block, BOTH, split_axis=0, concat_axis=0, tiled=True, axis_index_groups=cubes
    )
    block, last = lax.optimization_barrier((block.reshape(-1, block.shape[-1]), last))
    others = [swap_core(v) for v in (here, near, far, last)]
    weights = (gate_own, gate_other, up_own, up_other)
    all_rows = ((0, 1024),)
    by_x, by_y, by_z = exchange(block, "x", 1), exchange(block, "y", 1), exchange(block, "z", 1)
    carried = gather_products(place, ((all_rows, 0, 0),), (block,), weights, None, False)
    own, on_x = lax.optimization_barrier((carried[1], by_x))
    own, on_y = lax.optimization_barrier((own, by_y))
    own, on_z, *others[:2] = lax.optimization_barrier((own, by_z, *others[:2]))
    carried = (carried[0], own)
    by_xy, by_yz, by_xz = exchange(on_x, "y", 1), exchange(on_y, "z", 1), exchange(on_z, "x", 1)
    carried = gather_products(
        place,
        ((all_rows, 1, 0), (all_rows, 2, 0), (all_rows, 0, 1)),
        (by_x, by_y, by_z),
        weights,
        carried,
        False,
    )
    cuts = [value[low:high] for value, (low, high) in zip((by_xy, by_yz), HALVES)]
    own, cuts[0] = lax.optimization_barrier((carried[1], cuts[0]))
    own, cuts[1], others[2], others[3] = lax.optimization_barrier(
        (own, cuts[1], others[2], others[3])
    )
    carried = (carried[0], own)
    halves = [exchange(value, axis, 1) for value, axis in zip(cuts, "zx")]
    carried = gather_products(
        place,
        ((all_rows, 3, 0), (all_rows, 2, 1), (all_rows, 1, 1)),
        (by_xy, by_yz, by_xz),
        weights,
        carried,
        False,
    )
    hidden, index, own = gather_products(
        place, ((HALVES, 3, 1),), tuple(halves), weights, carried, True
    )
    spread = [hidden, exchange(hidden, "z", 0), exchange(hidden, "z", 1), shift_z(hidden, 2)]
    sums = down(place, index, spread, (w_down[0], near, far, last), others)
    lane_all = [
        [expert_of(y, x, core) * SIDE + z for z in range(SIDE) for y in range(SIDE) for x in range(SIDE)]
        for core in range(2)
    ]
    returned = lax.all_to_all(
        sums.reshape(SIDE * CHIPS, rows, quarter),
        BOTH,
        split_axis=0,
        concat_axis=0,
        tiled=True,
        axis_index_groups=lane_all,
    )
    routed = jnp.sum(returned.reshape(SIDE, CHIPS, rows, quarter).astype(F32), axis=1)
    routed = routed.transpose(1, 0, 2).reshape(rows, model)
    stream = own[:, :, :cols].transpose(1, 0, 2).reshape(rows, model) / norm_gain.astype(F32)
    return (stream + routed).astype(BF16)


def solution(mesh):
    return jax.shard_map(
        per_device,
        mesh=mesh,
        in_specs=(
            P(BOTH, None),
            P(BOTH, None, None, None),
            P(BOTH, None, None, None),
            P(BOTH, None, None),
            P(BOTH, None, None),
            P(BOTH, None, None),
            P(BOTH, None, None),
            P(BOTH),
            P(),
            P(None, "expert"),
            P(),
            P(BOTH, None),
            P(BOTH, None),
            P("expert", None, "tensor"),
            P("expert", None, "tensor"),
            P("expert", "tensor", None),
        ),
        out_specs=P(BOTH, None),
        check_vma=False,
    )
```

```python
import functools

import jax
import jax.numpy as jnp
from jax import lax
from jax.experimental import pallas as pl
from jax.experimental.pallas import tpu as pltpu
from jax.sharding import PartitionSpec as P

EPSILON = 1e-06
BOTH = ("expert", "tensor")
SIDE = 4
CHIPS = 16
HALVES = ((0, 512), (512, 1024))
F32 = jnp.float32
BF16 = jnp.bfloat16


def expert_of(y, x, core):
    return (y * SIDE + x) * 2 + core


def masks_of(core):
    return (1, 3) if core == 0 else (3, 1)


def swap_core(value):
    pairs = [(e, e ^ 1) for e in range(2 * CHIPS)]
    return lax.ppermute(value, "expert", pairs)


def shift_z(value, amount):
    pairs = [(z, (z + amount) % SIDE) for z in range(SIDE)]
    return lax.ppermute(value, "tensor", pairs)


def exchange(value, axis, turn):
    pairs = []
    for y in range(SIDE):
        for x in range(SIDE):
            for core in range(2):
                mask = masks_of(core)[turn]
                here = expert_of(y, x, core)
                if axis == "x":
                    pairs.append((here, expert_of(y, x ^ mask, core)))
                elif axis == "y":
                    pairs.append((here, expert_of(y ^ mask, x, core)))
                else:
                    for z in range(SIDE):
                        pairs.append((here * SIDE + z, here * SIDE + (z ^ mask)))
    return lax.ppermute(value, BOTH if axis == "z" else "expert", pairs)


def pairs_of(core):
    mask = masks_of(core)[0]
    return [(v, v ^ mask) for v in range(SIDE) if v < v ^ mask]


def attend_kernel(length_ref, q_ref, qr_ref, latent_ref, rope_ref, fresh_ref, fresh_rope_ref, out_ref, *, scale, heads):
    request = pl.program_id(0)
    query = q_ref[0]
    query_rope = qr_ref[0]
    latent = latent_ref[0]
    last = (((1,), (1,)), ((), ()))
    scores = lax.dot_general(query, latent, last, preferred_element_type=F32)
    scores = scores + jnp.dot(query_rope, rope_ref[0], preferred_element_type=F32)
    lane = lax.broadcasted_iota(jnp.int32, (1, scores.shape[1]), 1)
    scores = jnp.where(lane < length_ref[request], scores * scale, -1e30)
    fresh = fresh_ref[0]
    fresh_rope = fresh_rope_ref[0]
    recent = lax.dot_general(query, fresh, last, preferred_element_type=F32)
    recent = recent + lax.dot_general(query_rope, fresh_rope, last, preferred_element_type=F32)
    step = lax.broadcasted_iota(jnp.int32, recent.shape, 0) // heads
    place = lax.broadcasted_iota(jnp.int32, recent.shape, 1)
    recent = jnp.where(place <= step, recent * scale, -1e30)
    top = jnp.maximum(
        jnp.max(scores, axis=1, keepdims=True), jnp.max(recent, axis=1, keepdims=True)
    )
    weights = jnp.exp(scores - top)
    recent = jnp.exp(recent - top)
    total = jnp.sum(weights, axis=1, keepdims=True) + jnp.sum(recent, axis=1, keepdims=True)
    share = 1.0 / total
    mixed = jnp.dot((weights * share).astype(BF16), latent, preferred_element_type=F32)
    recent = (recent * share).astype(BF16).astype(F32)
    for n in range(fresh.shape[0]):
        mixed = mixed + recent[:, n : n + 1] * fresh[n : n + 1].astype(F32)
    out_ref[0] = mixed.astype(BF16)


def attention_heads(
    query_latent, query_rope, cache_latent, cache_rope, new_latent, new_rope, lengths, value_proj
):
    requests, steps, heads, latent = query_latent.shape
    rope = query_rope.shape[3]
    context = cache_latent.shape[1]
    rows = steps * heads
    scale = (value_proj.shape[2] + rope) ** (-0.5)
    whole = lambda *shape: pl.BlockSpec((1,) + shape, lambda i, s: (i, 0, 0))
    mixed = pl.pallas_call(
        functools.partial(attend_kernel, scale=scale, heads=heads),
        grid_spec=pltpu.PrefetchScalarGridSpec(
            num_scalar_prefetch=1,
            grid=(requests,),
            in_specs=[
                whole(rows, latent),
                whole(rows, rope),
                whole(context, latent),
                whole(rope, context),
                whole(steps, latent),
                whole(steps, rope),
            ],
            out_specs=whole(rows, latent),
        ),
        out_shape=jax.ShapeDtypeStruct((requests, rows, latent), BF16),
        cost_estimate=pl.CostEstimate(
            flops=2 * requests * rows * context * (2 * latent + rope),
            bytes_accessed=2 * requests * context * (latent + rope),
            transcendentals=requests * rows * context,
        ),
        compiler_params=pltpu.CompilerParams(vmem_limit_bytes=56 << 20),
    )(
        lengths,
        query_latent.reshape(requests, rows, latent),
        query_rope.reshape(requests, rows, rope),
        cache_latent,
        cache_rope,
        new_latent,
        new_rope,
    )
    head_values = jnp.einsum(
        "rshl,hlv->hrsv",
        mixed.reshape(requests, steps, heads, latent),
        value_proj,
        preferred_element_type=F32,
    )
    return head_values.astype(BF16).reshape(heads, requests * steps, -1)


def pack_kernel(
    heads_ref, residual_ref, ids_ref, gates_ref, out_ref, values, tail, done
):
    heads, rows, each = heads_ref.shape
    width = heads * each
    cols = residual_ref.shape[1] // CHIPS
    for head in range(heads):
        values[:, head * each : (head + 1) * each] = heads_ref[head]
    copies = [
        pltpu.make_async_copy(values, out_ref.at[chip, :, pl.ds(0, width)], done.at[chip])
        for chip in range(CHIPS)
    ]
    for copy in copies:
        copy.start()
    lane = lax.broadcasted_iota(jnp.int32, (rows, 128), 1)
    gates = jnp.zeros((rows, 128), F32)
    named = jnp.zeros((rows, 128), F32)
    for k in range(ids_ref.shape[1]):
        match = ids_ref[:, k : k + 1] == lane
        gates = gates + jnp.where(match, gates_ref[:, k : k + 1], 0.0)
        named = named + jnp.where(match, 1.0, 0.0)
    above = lax.broadcasted_iota(jnp.int32, (rows, rows), 1)
    below = above < lax.broadcasted_iota(jnp.int32, (rows, rows), 0)
    below = jnp.where(below, 1.0, 0.0).astype(BF16)
    rank = jnp.dot(below, named.astype(BF16), preferred_element_type=F32)
    rank = jnp.where(named > 0.5, rank, 8.0)
    high = gates.astype(BF16).astype(F32)
    low = gates - high
    for chip in range(CHIPS):
        at = 128 - 2 * chip
        picked = jnp.where(
            lane < 2,
            pltpu.roll(high, at % 128, 1),
            jnp.where(
                lane < 4, pltpu.roll(low, (at + 2) % 128, 1), pltpu.roll(rank, (at + 4) % 128, 1)
            ),
        )
        picked = jnp.where(lane < 6, picked, 0.0)[:, : 512 - cols]
        part = residual_ref[:, chip * cols : (chip + 1) * cols]
        tail[chip] = jnp.concatenate([part, picked.astype(BF16)], axis=1)
    last = pltpu.make_async_copy(
        tail, out_ref.at[:, :, pl.ds(width, tail.shape[2])], done.at[CHIPS]
    )
    last.start()
    for copy in copies + [last]:
        copy.wait()


def pack(heads, residual, ids, gates):
    count, rows, each = heads.shape
    width = count * each
    return pl.pallas_call(
        pack_kernel,
        in_specs=[pl.BlockSpec(memory_space=pltpu.VMEM)] * 4,
        out_specs=pl.BlockSpec(memory_space=pl.ANY),
        scratch_shapes=[
            pltpu.VMEM((rows, width), BF16),
            pltpu.VMEM((CHIPS, rows, 512), BF16),
            pltpu.SemaphoreType.DMA((CHIPS + 1,)),
        ],
        out_shape=jax.ShapeDtypeStruct((CHIPS, rows, width + 512), BF16),
        cost_estimate=pl.CostEstimate(
            flops=0, bytes_accessed=2 * CHIPS * rows * (width + 512), transcendentals=0
        ),
    )(heads, residual, ids, gates)


def project_kernel(
    place_ref, in_ref, own_ref, other_ref, gain_ref, out_ref, sum_own, sum_other, *, width
):
    step = pl.program_id(0)
    depth = own_ref.shape[0]

    @pl.when(step == 0)
    def _():
        sum_own[...] = jnp.zeros_like(sum_own)
        sum_other[...] = jnp.zeros_like(sum_other)

    heads = in_ref[:, pl.ds(pl.multiple_of(step * depth, 128), depth)]
    sum_own[...] += jnp.dot(heads, own_ref[...], preferred_element_type=F32)
    sum_other[...] += jnp.dot(heads, other_ref[...], preferred_element_type=F32)

    @pl.when(step == pl.num_programs(0) - 1)
    def _():
        first = place_ref[0] == 0
        own, other = sum_own[...], sum_other[...]
        left = jnp.where(first, own, other)
        right = jnp.where(first, other, own)
        both = jnp.concatenate([left, right], axis=1).astype(BF16).astype(F32)
        tail = in_ref[:, width:].astype(F32)
        cols = both.shape[1]
        stream = tail[:, :cols] + both
        square = jnp.sum(stream * stream, axis=1, keepdims=True)
        high = square.astype(BF16).astype(F32)
        low = square - high
        extra = tail[:, cols:]
        lane = lax.broadcasted_iota(jnp.int32, extra.shape, 1)
        extra = jnp.where(lane == 6, high, jnp.where(lane == 7, low, extra))
        stream = stream * gain_ref[0].astype(F32)
        value = jnp.concatenate([stream, extra], axis=1).astype(BF16)
        for i in range(out_ref.shape[0]):
            out_ref[i] = value


def project(place, landed, own, other, gain):
    rows, total = landed.shape
    width, cols = own.shape
    steps = 4
    depth = width // steps
    out = total - width
    return pl.pallas_call(
        functools.partial(project_kernel, width=width),
        grid_spec=pltpu.PrefetchScalarGridSpec(
            num_scalar_prefetch=1,
            grid=(steps,),
            in_specs=[
                pl.BlockSpec((rows, total), lambda i, s: (0, 0)),
                pl.BlockSpec((depth, cols), lambda i, s: (i, 0)),
                pl.BlockSpec((depth, cols), lambda i, s: (i, 0)),
                pl.BlockSpec((1, 1, 2 * cols), lambda i, s: (s[1], 0, 0)),
            ],
            out_specs=pl.BlockSpec((8, rows, out), lambda i, s: (0, 0, 0)),
            scratch_shapes=[pltpu.VMEM((rows, cols), F32)] * 2,
        ),
        out_shape=jax.ShapeDtypeStruct((8, rows, out), BF16),
        cost_estimate=pl.CostEstimate(
            flops=4 * rows * width * cols, bytes_accessed=4 * width * cols, transcendentals=0
        ),
        compiler_params=pltpu.CompilerParams(vmem_limit_bytes=24 << 20),
    )(place, landed, own, other, gain.reshape(CHIPS, 1, 2 * cols))


def gather_kernel(place_ref, *refs, units, first, done, model):
    counts = [len(rows) for rows, _, _ in units]
    blocks, refs = refs[: sum(counts)], refs[sum(counts) :]
    sources, refs = refs[:4], refs[4:]
    final = done == 1
    if final:
        total_in, sums_in, hidden_ref, index_ref, total, tokens, weight, arrived = refs
    else:
        if not first:
            (total_in, own_in), refs = refs[:2], refs[2:]
        total, own_ref, refs = refs[0], refs[1], refs[2:]
        if done == 0:
            (sums_ref, index_ref), refs = refs[:2], refs[2:]
        tokens, weight, arrived = refs
    part = sources[0].shape[1]
    cols = model // CHIPS
    wide = blocks[0].shape[1]
    width = 4 * part
    spare = wide - cols

    def fetch(unit, near):
        chip = place_ref[units[unit][1] * 4 + near]
        source = pl.ds(pl.multiple_of(chip * cols, 64), cols)
        return [
            pltpu.make_async_copy(
                ref.at[source],
                weight.at[unit, pl.ds(near * wide, cols), pl.ds(i * part, part)],
                arrived.at[unit, near, i],
            )
            for i, ref in enumerate(sources)
        ]

    for unit in range(len(units)):
        for near in range(4):
            for copy in fetch(unit, near):
                copy.start()
    for unit in range(len(units)):
        for near in range(4):
            weight[unit, near * wide + cols : (near + 1) * wide] = jnp.zeros((spare, width), BF16)
    if first:
        total[...] = jnp.zeros_like(total)
        own_ref[...] = jnp.zeros_like(own_ref)
    elif final:
        total[1] = total_in[1]
    else:
        total[...] = total_in[...]
        own_ref[...] = own_in[...]

    chip = place_ref[20]
    start = pl.multiple_of(place_ref[24] * 128 + (chip // 2) * 16, 16)
    for unit, (rows, far, far_z) in enumerate(units):
        here, blocks = blocks[: len(rows)], blocks[len(rows) :]
        for (low, high), ref in zip(rows, here):
            row = low
            while row < high:
                count = min(128 - row % 128, high - row)
                near_z, near = divmod(row // 128, 4)
                at = near_z * 128 + row % 128
                tokens[at : at + count, near * wide : (near + 1) * wide] = ref[
                    row - low : row - low + count
                ]
                row += count
        extra = None
        for near in range(4):
            term = tokens[:, near * wide + cols : (near + 1) * wide].astype(F32)
            extra = term if extra is None else extra + term
            if far_z == 0:
                mine = tokens[pl.ds(start, 16), near * wide : (near + 1) * wide].astype(F32)
                own_ref[pl.ds(place_ref[far * 4 + near], 1)] = jnp.where(
                    lax.rem(chip, 2) == 0, mine[:8], mine[8:]
                )[None]
            for copy in fetch(unit, near):
                copy.wait()
        if far == 0:
            at = pl.multiple_of(place_ref[23] * wide + cols // 128 * 128, 128)
            total[far_z, :, width + spare :] = tokens[:, pl.ds(at, 128)][:, cols % 128 :].astype(
                F32
            )
        total[far_z, :, width : width + spare] += extra
        total[far_z, :, :width] += jnp.dot(
            tokens[...], weight[unit], preferred_element_type=F32
        )
    if done is None:
        return

    group = lax.broadcasted_iota(jnp.int32, (128, 1), 0) // 8
    slots = 4 * 4 * CHIPS
    lanes = lax.broadcasted_iota(jnp.int32, (1, slots), 1)
    even = place_ref[21] == 0
    extra = total[done, :, width:]
    square = (extra[:, 6:7] + extra[:, 7:8]) * (1.0 / model)
    inverse = lax.rsqrt(square + EPSILON)
    names = extra[:, spare:]
    bases = jnp.concatenate(
        [group * 4 + place_ref[16 + done * 2 + i] * (4 * CHIPS) for i in range(2)], axis=0
    )
    gates = [names[:, i : i + 1] + names[:, 2 + i : 3 + i] for i in range(2)]
    ranks = [names[:, 4 + i : 5 + i].astype(jnp.int32) for i in range(2)]
    for i in range(2):
        gate = total[done, :, i * part : (i + 1) * part] * inverse
        up = total[done, :, (2 + i) * part : (3 + i) * part] * inverse
        share = jnp.where(even, gates[i], gates[1 - i])
        rank = jnp.where(even, ranks[i], ranks[1 - i])
        value = gate * (1.0 / (1.0 + jnp.exp(-gate))) * up * share
        place_index = jnp.where(rank < 4, bases + rank, -1)
        index_ref[:, i : i + 1] = place_index
        hot = (place_index == lanes).astype(BF16)
        term = lax.dot_general(
            hot, value.astype(BF16), (((0,), (0,)), ((), ())), preferred_element_type=F32
        )
        if final:
            hidden_ref[i] = (sums_in[i] + term).astype(BF16)
        else:
            sums_ref[i] = term


def gather_products(place, units, blocks, weights, carried, done=None):
    model, part = weights[0].shape
    wide = blocks[0].shape[1]
    width = 4 * part
    tok = SIDE * 128
    spare = wide - model // CHIPS
    whole = lambda *shape: pl.BlockSpec(shape, lambda i, s: (0,) * len(shape))
    total_shape = (2, tok // 2, width + 2 * spare)
    own_shape = (CHIPS, 8, wide)
    scratch = [
        pltpu.VMEM((tok // 2, 4 * wide), BF16),
        pltpu.VMEM((len(units), 4 * wide, width), BF16),
        pltpu.SemaphoreType.DMA((len(units), 4, 4)),
    ]
    sums_shape = (2, tok // 2, part)
    index_out = ((tok // 2, 2), jnp.int32)
    carried_shapes = (total_shape, own_shape)
    if done == 1:
        outs = [(sums_shape, BF16), index_out]
        scratch = [pltpu.VMEM(total_shape, F32)] + scratch
        carried_shapes = (total_shape, sums_shape)
    else:
        outs = [(total_shape, F32), (own_shape, F32)]
        if done == 0:
            outs += [(sums_shape, F32), index_out]
    return pl.pallas_call(
        functools.partial(
            gather_kernel, units=units, first=carried is None, done=done, model=model
        ),
        grid_spec=pltpu.PrefetchScalarGridSpec(
            num_scalar_prefetch=1,
            grid=(1,),
            in_specs=[whole(*b.shape) for b in blocks]
            + [pl.BlockSpec(memory_space=pltpu.HBM)] * 4
            + ([] if carried is None else [whole(*shape) for shape in carried_shapes]),
            out_specs=[whole(*shape) for shape, _ in outs],
            scratch_shapes=scratch,
        ),
        out_shape=[jax.ShapeDtypeStruct(shape, kind) for shape, kind in outs],
        cost_estimate=pl.CostEstimate(
            flops=len(units) * tok * 4 * wide * width,
            bytes_accessed=len(units) * 8 * wide * width,
            transcendentals=0,
        ),
        compiler_params=pltpu.CompilerParams(vmem_limit_bytes=44 << 20),
    )(place, *blocks, *weights, *(() if carried is None else carried))


def down_kernel(place_ref, low_ref, high_ref, *refs):
    hidden, own, other = refs[:4], refs[4:8], refs[8:12]
    out_ref, values, weight, sums, arrived = refs[12:]
    slots = values.shape[1]
    width = weight.shape[2]
    part = weight.shape[1] // 4
    start = pl.multiple_of(place_ref[22] * width, 128)

    def fetch(i):
        copies = []
        for k in range(4):
            source = other[(0, 2, 1, 3)[k]]
            if i == 0:
                source = own[k].at[:, pl.ds(start, width)] if k == 0 else own[k]
            rows = pl.ds(k * part, part)
            copies.append((source, weight.at[i, rows], arrived.at[i, 0, k]))
            copies.append((hidden[k].at[i], values.at[i, :, rows], arrived.at[i, 1, k]))
        return [pltpu.make_async_copy(*copy) for copy in copies]

    for i in range(2):
        for copy in fetch(i):
            copy.start()
    lanes = lax.broadcasted_iota(jnp.int32, (1, slots), 1)
    index = jnp.concatenate([low_ref[...], high_ref[...]], axis=0)
    hots = [(index[:, i : i + 1] == lanes).astype(BF16) for i in range(2)]
    for i in range(2):
        for copy in fetch(i):
            copy.wait()
        sums[i * slots : (i + 1) * slots] = jnp.dot(
            values[i], weight[i], preferred_element_type=F32
        ).astype(BF16)
    result = jnp.dot(
        jnp.concatenate(hots, axis=1), sums[...], preferred_element_type=F32
    ).astype(BF16)
    for i in range(4):
        at = pl.multiple_of(place_ref[16 + i] * 128, 128)
        out_ref[pl.ds(at, 128), :] = result[i * 128 : (i + 1) * 128]


def down(place, index_low, index_high, hidden, own, other):
    half = index_low.shape[0]
    slots, part = hidden[0].shape[1:]
    width = own[1].shape[1]
    whole = lambda *shape: pl.BlockSpec(shape, lambda i, s: (0,) * len(shape))
    return pl.pallas_call(
        down_kernel,
        grid_spec=pltpu.PrefetchScalarGridSpec(
            num_scalar_prefetch=1,
            grid=(1,),
            in_specs=[whole(half, 2)] * 2 + [pl.BlockSpec(memory_space=pl.ANY)] * 12,
            out_specs=whole(2 * half, width),
            scratch_shapes=[
                pltpu.VMEM((2, slots, 4 * part), BF16),
                pltpu.VMEM((2, 4 * part, width), BF16),
                pltpu.VMEM((2 * slots, width), BF16),
                pltpu.SemaphoreType.DMA((2, 2, 4)),
            ],
        ),
        out_shape=jax.ShapeDtypeStruct((2 * half, width), BF16),
        cost_estimate=pl.CostEstimate(
            flops=24 * half * part * width, bytes_accessed=16 * part * width, transcendentals=0
        ),
        compiler_params=pltpu.CompilerParams(vmem_limit_bytes=32 << 20),
    )(place, index_low, index_high, *hidden, *own, *other)


def per_device(
    residual,
    query_latent,
    query_rope,
    cache_latent,
    cache_rope,
    new_latent,
    new_rope,
    lengths,
    value_proj,
    out_proj,
    norm_gain,
    expert_ids,
    expert_gates,
    w_gate,
    w_up,
    w_down,
):
    rows, model = residual.shape
    expert = lax.axis_index("expert")
    plane = lax.axis_index("tensor")
    core = expert % 2
    chip = expert // 2
    first = jnp.where(core == 0, 1, 3)
    second = 4 - first
    pair = lambda v: (jnp.minimum(v, v ^ first), jnp.maximum(v, v ^ first))
    row, column = chip // SIDE, chip % SIDE
    table = []
    for far_y in range(2):
        for far_x in range(2):
            for near_y in range(2):
                for near_x in range(2):
                    table.append(
                        pair(row ^ (second * far_y))[near_y] * SIDE
                        + pair(column ^ (second * far_x))[near_x]
                    )
    for far_z in range(2):
        for near_z in range(2):
            table.append(pair(plane ^ (second * far_z))[near_z])
    is_high = lambda v: jnp.where(v == pair(v)[1], 1, 0)
    table += [chip, core, plane, is_high(row) * 2 + is_high(column), is_high(plane)]
    place = jnp.stack([jnp.asarray(v, jnp.int32) for v in table])

    quarter = model // SIDE
    half = w_down.shape[1]
    cut = lambda v, z: lax.dynamic_slice(v, (0, z * quarter), (half, quarter))
    lengths, passed, near = lax.optimization_barrier(
        (lengths, cut(w_down[0], plane ^ first ^ second), cut(w_down[0], plane ^ first))
    )
    passed, near = exchange(passed, "z", 0), exchange(near, "z", 0)
    out_other = swap_core(out_proj.T)
    gate_own, up_own = w_gate[0], w_up[0]
    gate_other, up_other = swap_core(gate_own), swap_core(up_own)

    heads = attention_heads(
        query_latent,
        query_rope,
        cache_latent,
        cache_rope,
        new_latent,
        new_rope,
        lengths,
        value_proj,
    )
    cols = model // CHIPS
    sent = pack(heads, residual, expert_ids, expert_gates)
    sent, out_other, gate_other, up_other, passed, late_down = lax.optimization_barrier(
        (sent, out_other, gate_other, up_other, passed, w_down[0])
    )
    here = cut(late_down, plane)
    far = exchange(cut(late_down, plane ^ second), "z", 1)
    lane_plane = [
        [expert_of(y, x, core) for y in range(SIDE) for x in range(SIDE)] for core in range(2)
    ]
    landed = lax.all_to_all(
        sent, "expert", split_axis=0, concat_axis=0, tiled=True, axis_index_groups=lane_plane
    )
    landed, near, far = lax.optimization_barrier((landed, near, far))
    block = project(
        jnp.stack([core, chip]).astype(jnp.int32),
        landed.reshape(CHIPS * rows, -1),
        out_proj,
        out_other.T,
        norm_gain,
    )
    last = exchange(passed, "z", 1)
    cubes = [
        [expert_of(y, x, core) * SIDE + z for z in z_pair for y in y_pair for x in x_pair]
        for core in range(2)
        for z_pair in pairs_of(core)
        for y_pair in pairs_of(core)
        for x_pair in pairs_of(core)
    ]
    block = lax.all_to_all(
        block, BOTH, split_axis=0, concat_axis=0, tiled=True, axis_index_groups=cubes
    )
    block, last = lax.optimization_barrier((block.reshape(-1, block.shape[-1]), last))
    others = [swap_core(v) for v in (here, near, far, last)]
    weights = (gate_own, gate_other, up_own, up_other)
    all_rows = ((0, 1024),)
    by_x, by_y, by_z = exchange(block, "x", 1), exchange(block, "y", 1), exchange(block, "z", 1)
    carried = gather_products(place, ((all_rows, 0, 0),), (block,), weights, None)
    own, on_x = lax.optimization_barrier((carried[1], by_x))
    own, on_y = lax.optimization_barrier((own, by_y))
    own, on_z, *others[:2] = lax.optimization_barrier((own, by_z, *others[:2]))
    carried = (carried[0], own)
    by_xy, by_yz, by_xz = exchange(on_x, "y", 1), exchange(on_y, "z", 1), exchange(on_z, "x", 1)
    carried = gather_products(
        place,
        ((all_rows, 1, 0), (all_rows, 2, 0), (all_rows, 0, 1)),
        (by_x, by_y, by_z),
        weights,
        carried,
    )
    cuts = [value[low:high] for value, (low, high) in zip((by_xy, by_yz), HALVES)]
    own, cuts[0] = lax.optimization_barrier((carried[1], cuts[0]))
    own, cuts[1], others[2], others[3] = lax.optimization_barrier(
        (own, cuts[1], others[2], others[3])
    )
    carried = (carried[0], own)
    halves = [exchange(value, axis, 1) for value, axis in zip(cuts, "zx")]
    total, own, part_sums, index_low = gather_products(
        place,
        ((all_rows, 3, 0), (all_rows, 2, 1), (all_rows, 1, 1)),
        (by_xy, by_yz, by_xz),
        weights,
        carried,
        0,
    )
    hidden, index_high = gather_products(
        place, ((HALVES, 3, 1),), tuple(halves), weights, (total, part_sums), 1
    )
    spread = [hidden, exchange(hidden, "z", 0), exchange(hidden, "z", 1), shift_z(hidden, 2)]
    sums = down(place, index_low, index_high, spread, (w_down[0], near, far, last), others)
    lane_all = [
        [expert_of(y, x, core) * SIDE + z for z in range(SIDE) for y in range(SIDE) for x in range(SIDE)]
        for core in range(2)
    ]
    returned = lax.all_to_all(
        sums.reshape(SIDE * CHIPS, rows, quarter),
        BOTH,
        split_axis=0,
        concat_axis=0,
        tiled=True,
        axis_index_groups=lane_all,
    )
    routed = jnp.sum(returned.reshape(SIDE, CHIPS, rows, quarter).astype(F32), axis=1)
    routed = routed.transpose(1, 0, 2).reshape(rows, model)
    stream = own[:, :, :cols].transpose(1, 0, 2).reshape(rows, model) / norm_gain.astype(F32)
    return (stream + routed).astype(BF16)


def solution(mesh):
    return jax.shard_map(
        per_device,
        mesh=mesh,
        in_specs=(
            P(BOTH, None),
            P(BOTH, None, None, None),
            P(BOTH, None, None, None),
            P(BOTH, None, None),
            P(BOTH, None, None),
            P(BOTH, None, None),
            P(BOTH, None, None),
            P(BOTH),
            P(),
            P(None, "expert"),
            P(),
            P(BOTH, None),
            P(BOTH, None),
            P("expert", None, "tensor"),
            P("expert", None, "tensor"),
            P("expert", "tensor", None),
        ),
        out_specs=P(BOTH, None),
        check_vma=False,
    )
```

```python
import functools

import jax
import jax.numpy as jnp
from jax import lax
from jax.experimental import pallas as pl
from jax.experimental.pallas import tpu as pltpu
from jax.sharding import PartitionSpec as P

EPSILON = 1e-06
BOTH = ("expert", "tensor")
SIDE = 4
CHIPS = 16
HALVES = ((0, 512), (512, 1024))
F32 = jnp.float32
BF16 = jnp.bfloat16


def expert_of(y, x, core):
    return (y * SIDE + x) * 2 + core


def masks_of(core):
    return (1, 3) if core == 0 else (3, 1)


def swap_core(value):
    pairs = [(e, e ^ 1) for e in range(2 * CHIPS)]
    return lax.ppermute(value, "expert", pairs)


def shift_z(value, amount):
    pairs = [(z, (z + amount) % SIDE) for z in range(SIDE)]
    return lax.ppermute(value, "tensor", pairs)


def exchange(value, axis, turn):
    pairs = []
    for y in range(SIDE):
        for x in range(SIDE):
            for core in range(2):
                mask = masks_of(core)[turn]
                here = expert_of(y, x, core)
                if axis == "x":
                    pairs.append((here, expert_of(y, x ^ mask, core)))
                elif axis == "y":
                    pairs.append((here, expert_of(y ^ mask, x, core)))
                else:
                    for z in range(SIDE):
                        pairs.append((here * SIDE + z, here * SIDE + (z ^ mask)))
    return lax.ppermute(value, BOTH if axis == "z" else "expert", pairs)


def pairs_of(core):
    mask = masks_of(core)[0]
    return [(v, v ^ mask) for v in range(SIDE) if v < v ^ mask]


def attend_kernel(length_ref, q_ref, qr_ref, latent_ref, rope_ref, fresh_ref, fresh_rope_ref, out_ref, *, scale, heads):
    request = pl.program_id(0)
    query = q_ref[0]
    query_rope = qr_ref[0]
    latent = latent_ref[0]
    last = (((1,), (1,)), ((), ()))
    scores = lax.dot_general(query, latent, last, preferred_element_type=F32)
    scores = scores + jnp.dot(query_rope, rope_ref[0], preferred_element_type=F32)
    lane = lax.broadcasted_iota(jnp.int32, (1, scores.shape[1]), 1)
    scores = jnp.where(lane < length_ref[request], scores * scale, -1e30)
    fresh = fresh_ref[0]
    fresh_rope = fresh_rope_ref[0]
    recent = lax.dot_general(query, fresh, last, preferred_element_type=F32)
    recent = recent + lax.dot_general(query_rope, fresh_rope, last, preferred_element_type=F32)
    step = lax.broadcasted_iota(jnp.int32, recent.shape, 0) // heads
    place = lax.broadcasted_iota(jnp.int32, recent.shape, 1)
    recent = jnp.where(place <= step, recent * scale, -1e30)
    top = jnp.maximum(
        jnp.max(scores, axis=1, keepdims=True), jnp.max(recent, axis=1, keepdims=True)
    )
    weights = jnp.exp(scores - top)
    recent = jnp.exp(recent - top)
    total = jnp.sum(weights, axis=1, keepdims=True) + jnp.sum(recent, axis=1, keepdims=True)
    share = 1.0 / total
    mixed = jnp.dot((weights * share).astype(BF16), latent, preferred_element_type=F32)
    recent = (recent * share).astype(BF16).astype(F32)
    for n in range(fresh.shape[0]):
        mixed = mixed + recent[:, n : n + 1] * fresh[n : n + 1].astype(F32)
    out_ref[0] = mixed.astype(BF16)


def attention_heads(
    query_latent, query_rope, cache_latent, cache_rope, new_latent, new_rope, lengths, value_proj
):
    requests, steps, heads, latent = query_latent.shape
    rope = query_rope.shape[3]
    context = cache_latent.shape[1]
    rows = steps * heads
    scale = (value_proj.shape[2] + rope) ** (-0.5)
    whole = lambda *shape: pl.BlockSpec((1,) + shape, lambda i, s: (i, 0, 0))
    mixed = pl.pallas_call(
        functools.partial(attend_kernel, scale=scale, heads=heads),
        grid_spec=pltpu.PrefetchScalarGridSpec(
            num_scalar_prefetch=1,
            grid=(requests,),
            in_specs=[
                whole(rows, latent),
                whole(rows, rope),
                whole(context, latent),
                whole(rope, context),
                whole(steps, latent),
                whole(steps, rope),
            ],
            out_specs=whole(rows, latent),
        ),
        out_shape=jax.ShapeDtypeStruct((requests, rows, latent), BF16),
        cost_estimate=pl.CostEstimate(
            flops=2 * requests * rows * context * (2 * latent + rope),
            bytes_accessed=2 * requests * context * (latent + rope),
            transcendentals=requests * rows * context,
        ),
        compiler_params=pltpu.CompilerParams(vmem_limit_bytes=56 << 20),
    )(
        lengths,
        query_latent.reshape(requests, rows, latent),
        query_rope.reshape(requests, rows, rope),
        cache_latent,
        cache_rope,
        new_latent,
        new_rope,
    )
    head_values = jnp.einsum(
        "rshl,hlv->hrsv",
        mixed.reshape(requests, steps, heads, latent),
        value_proj,
        preferred_element_type=F32,
    )
    return head_values.astype(BF16).reshape(heads, requests * steps, -1)


def pack_kernel(heads_ref, residual_ref, ids_ref, gates_ref, out_ref):
    heads, rows, each = heads_ref.shape
    width = heads * each
    cols = residual_ref.shape[1] // CHIPS
    values = jnp.concatenate([heads_ref[head] for head in range(heads)], axis=1)
    lane = lax.broadcasted_iota(jnp.int32, (rows, 128), 1)
    gates = jnp.zeros((rows, 128), F32)
    named = jnp.zeros((rows, 128), F32)
    for k in range(ids_ref.shape[1]):
        match = ids_ref[:, k : k + 1] == lane
        gates = gates + jnp.where(match, gates_ref[:, k : k + 1], 0.0)
        named = named + jnp.where(match, 1.0, 0.0)
    above = lax.broadcasted_iota(jnp.int32, (rows, rows), 1)
    below = above < lax.broadcasted_iota(jnp.int32, (rows, rows), 0)
    below = jnp.where(below, 1.0, 0.0).astype(BF16)
    rank = jnp.dot(below, named.astype(BF16), preferred_element_type=F32)
    rank = jnp.where(named > 0.5, rank, 8.0)
    high = gates.astype(BF16).astype(F32)
    low = gates - high
    for chip in range(CHIPS):
        at = 128 - 2 * chip
        picked = jnp.where(
            lane < 2,
            pltpu.roll(high, at % 128, 1),
            jnp.where(
                lane < 4, pltpu.roll(low, (at + 2) % 128, 1), pltpu.roll(rank, (at + 4) % 128, 1)
            ),
        )
        picked = jnp.where(lane < 6, picked, 0.0)[:, : 512 - cols]
        part = residual_ref[:, chip * cols : (chip + 1) * cols]
        out_ref[chip, :, :width] = values
        out_ref[chip, :, width:] = jnp.concatenate([part, picked.astype(BF16)], axis=1)


def pack(heads, residual, ids, gates):
    count, rows, each = heads.shape
    width = count * each
    return pl.pallas_call(
        pack_kernel,
        in_specs=[pl.BlockSpec(memory_space=pltpu.VMEM)] * 4,
        out_specs=pl.BlockSpec(memory_space=pltpu.VMEM),
        out_shape=jax.ShapeDtypeStruct((CHIPS, rows, width + 512), BF16),
        cost_estimate=pl.CostEstimate(
            flops=0, bytes_accessed=2 * CHIPS * rows * (width + 512), transcendentals=0
        ),
    )(heads, residual, ids, gates)


def project_kernel(
    place_ref, in_ref, own_ref, other_ref, gain_ref, out_ref, sum_own, sum_other, *, width
):
    step = pl.program_id(0)
    depth = own_ref.shape[0]

    @pl.when(step == 0)
    def _():
        sum_own[...] = jnp.zeros_like(sum_own)
        sum_other[...] = jnp.zeros_like(sum_other)

    heads = in_ref[:, pl.ds(pl.multiple_of(step * depth, 128), depth)]
    sum_own[...] += jnp.dot(heads, own_ref[...], preferred_element_type=F32)
    sum_other[...] += jnp.dot(heads, other_ref[...], preferred_element_type=F32)

    @pl.when(step == pl.num_programs(0) - 1)
    def _():
        first = place_ref[0] == 0
        own, other = sum_own[...], sum_other[...]
        left = jnp.where(first, own, other)
        right = jnp.where(first, other, own)
        both = jnp.concatenate([left, right], axis=1).astype(BF16).astype(F32)
        tail = in_ref[:, width:].astype(F32)
        cols = both.shape[1]
        stream = tail[:, :cols] + both
        square = jnp.sum(stream * stream, axis=1, keepdims=True)
        high = square.astype(BF16).astype(F32)
        low = square - high
        extra = tail[:, cols:]
        lane = lax.broadcasted_iota(jnp.int32, extra.shape, 1)
        extra = jnp.where(lane == 6, high, jnp.where(lane == 7, low, extra))
        stream = stream * gain_ref[0].astype(F32)
        value = jnp.concatenate([stream, extra], axis=1).astype(BF16)
        for i in range(out_ref.shape[0]):
            out_ref[i] = value


def project(place, landed, own, other, gain):
    rows, total = landed.shape
    width, cols = own.shape
    steps = 4
    depth = width // steps
    out = total - width
    return pl.pallas_call(
        functools.partial(project_kernel, width=width),
        grid_spec=pltpu.PrefetchScalarGridSpec(
            num_scalar_prefetch=1,
            grid=(steps,),
            in_specs=[
                pl.BlockSpec((rows, total), lambda i, s: (0, 0)),
                pl.BlockSpec((depth, cols), lambda i, s: (i, 0)),
                pl.BlockSpec((depth, cols), lambda i, s: (i, 0)),
                pl.BlockSpec((1, 1, 2 * cols), lambda i, s: (s[1], 0, 0)),
            ],
            out_specs=pl.BlockSpec((8, rows, out), lambda i, s: (0, 0, 0)),
            scratch_shapes=[pltpu.VMEM((rows, cols), F32)] * 2,
        ),
        out_shape=jax.ShapeDtypeStruct((8, rows, out), BF16),
        cost_estimate=pl.CostEstimate(
            flops=4 * rows * width * cols, bytes_accessed=4 * width * cols, transcendentals=0
        ),
        compiler_params=pltpu.CompilerParams(vmem_limit_bytes=24 << 20),
    )(place, landed, own, other, gain.reshape(CHIPS, 1, 2 * cols))


def gather_kernel(place_ref, *refs, units, first, done, model):
    counts = [len(rows) for rows, _, _ in units]
    blocks, refs = refs[: sum(counts)], refs[sum(counts) :]
    sources, refs = refs[:4], refs[4:]
    final = done == 1
    if final:
        total_in, sums_in, hidden_ref, index_ref, total, tokens, weight, arrived = refs
    else:
        if not first:
            (total_in, own_in), refs = refs[:2], refs[2:]
        total, own_ref, refs = refs[0], refs[1], refs[2:]
        if done == 0:
            (sums_ref, index_ref), refs = refs[:2], refs[2:]
        tokens, weight, arrived = refs
    part = sources[0].shape[1]
    cols = model // CHIPS
    wide = blocks[0].shape[1]
    width = 4 * part
    spare = wide - cols

    def fetch(unit, near):
        chip = place_ref[units[unit][1] * 4 + near]
        source = pl.ds(pl.multiple_of(chip * cols, 64), cols)
        return [
            pltpu.make_async_copy(
                ref.at[source],
                weight.at[unit, pl.ds(near * wide, cols), pl.ds(i * part, part)],
                arrived.at[unit, near, i],
            )
            for i, ref in enumerate(sources)
        ]

    for unit in range(len(units)):
        for near in range(4):
            for copy in fetch(unit, near):
                copy.start()
    for unit in range(len(units)):
        for near in range(4):
            weight[unit, near * wide + cols : (near + 1) * wide] = jnp.zeros((spare, width), BF16)
    if first:
        total[...] = jnp.zeros_like(total)
        own_ref[...] = jnp.zeros_like(own_ref)
    elif final:
        total[1] = total_in[1]
    else:
        total[...] = total_in[...]
        own_ref[...] = own_in[...]

    chip = place_ref[20]
    start = pl.multiple_of(place_ref[24] * 128 + (chip // 2) * 16, 16)
    for unit, (rows, far, far_z) in enumerate(units):
        here, blocks = blocks[: len(rows)], blocks[len(rows) :]
        for (low, high), ref in zip(rows, here):
            row = low
            while row < high:
                count = min(128 - row % 128, high - row)
                near_z, near = divmod(row // 128, 4)
                at = near_z * 128 + row % 128
                tokens[at : at + count, near * wide : (near + 1) * wide] = ref[
                    row - low : row - low + count
                ]
                row += count
        extra = None
        for near in range(4):
            term = tokens[:, near * wide + cols : (near + 1) * wide].astype(F32)
            extra = term if extra is None else extra + term
            if far_z == 0:
                mine = tokens[pl.ds(start, 16), near * wide : (near + 1) * wide].astype(F32)
                own_ref[pl.ds(place_ref[far * 4 + near], 1)] = jnp.where(
                    lax.rem(chip, 2) == 0, mine[:8], mine[8:]
                )[None]
            for copy in fetch(unit, near):
                copy.wait()
        if far == 0:
            at = pl.multiple_of(place_ref[23] * wide + cols // 128 * 128, 128)
            total[far_z, :, width + spare :] = tokens[:, pl.ds(at, 128)][:, cols % 128 :].astype(
                F32
            )
        total[far_z, :, width : width + spare] += extra
        total[far_z, :, :width] += jnp.dot(
            tokens[...], weight[unit], preferred_element_type=F32
        )
    if done is None:
        return

    group = lax.broadcasted_iota(jnp.int32, (128, 1), 0) // 8
    slots = 4 * 4 * CHIPS
    lanes = lax.broadcasted_iota(jnp.int32, (1, slots), 1)
    even = place_ref[21] == 0
    extra = total[done, :, width:]
    square = (extra[:, 6:7] + extra[:, 7:8]) * (1.0 / model)
    inverse = lax.rsqrt(square + EPSILON)
    names = extra[:, spare:]
    bases = jnp.concatenate(
        [group * 4 + place_ref[16 + done * 2 + i] * (4 * CHIPS) for i in range(2)], axis=0
    )
    gates = [names[:, i : i + 1] + names[:, 2 + i : 3 + i] for i in range(2)]
    ranks = [names[:, 4 + i : 5 + i].astype(jnp.int32) for i in range(2)]
    for i in range(2):
        gate = total[done, :, i * part : (i + 1) * part] * inverse
        up = total[done, :, (2 + i) * part : (3 + i) * part] * inverse
        share = jnp.where(even, gates[i], gates[1 - i])
        rank = jnp.where(even, ranks[i], ranks[1 - i])
        value = gate * (1.0 / (1.0 + jnp.exp(-gate))) * up * share
        place_index = jnp.where(rank < 4, bases + rank, -1)
        index_ref[:, i : i + 1] = place_index
        hot = (place_index == lanes).astype(BF16)
        term = lax.dot_general(
            hot, value.astype(BF16), (((0,), (0,)), ((), ())), preferred_element_type=F32
        )
        if final:
            hidden_ref[i] = (sums_in[i] + term).astype(BF16)
        else:
            sums_ref[i] = term


def gather_products(place, units, blocks, weights, carried, done=None):
    model, part = weights[0].shape
    wide = blocks[0].shape[1]
    width = 4 * part
    tok = SIDE * 128
    spare = wide - model // CHIPS
    whole = lambda *shape: pl.BlockSpec(shape, lambda i, s: (0,) * len(shape))
    total_shape = (2, tok // 2, width + 2 * spare)
    own_shape = (CHIPS, 8, wide)
    scratch = [
        pltpu.VMEM((tok // 2, 4 * wide), BF16),
        pltpu.VMEM((len(units), 4 * wide, width), BF16),
        pltpu.SemaphoreType.DMA((len(units), 4, 4)),
    ]
    sums_shape = (2, tok // 2, part)
    index_out = ((tok // 2, 2), jnp.int32)
    carried_shapes = (total_shape, own_shape)
    if done == 1:
        outs = [(sums_shape, BF16), index_out]
        scratch = [pltpu.VMEM(total_shape, F32)] + scratch
        carried_shapes = (total_shape, sums_shape)
    else:
        outs = [(total_shape, F32), (own_shape, F32)]
        if done == 0:
            outs += [(sums_shape, F32), index_out]
    return pl.pallas_call(
        functools.partial(
            gather_kernel, units=units, first=carried is None, done=done, model=model
        ),
        grid_spec=pltpu.PrefetchScalarGridSpec(
            num_scalar_prefetch=1,
            grid=(1,),
            in_specs=[whole(*b.shape) for b in blocks]
            + [pl.BlockSpec(memory_space=pltpu.HBM)] * 4
            + ([] if carried is None else [whole(*shape) for shape in carried_shapes]),
            out_specs=[whole(*shape) for shape, _ in outs],
            scratch_shapes=scratch,
        ),
        out_shape=[jax.ShapeDtypeStruct(shape, kind) for shape, kind in outs],
        cost_estimate=pl.CostEstimate(
            flops=len(units) * tok * 4 * wide * width,
            bytes_accessed=len(units) * 8 * wide * width,
            transcendentals=0,
        ),
        compiler_params=pltpu.CompilerParams(vmem_limit_bytes=44 << 20),
    )(place, *blocks, *weights, *(() if carried is None else carried))


def down_kernel(place_ref, low_ref, high_ref, *refs):
    hidden, own, other = refs[:4], refs[4:8], refs[8:12]
    out_ref, values, weight, sums, arrived = refs[12:]
    slots = values.shape[1]
    width = weight.shape[2]
    part = weight.shape[1] // 4
    start = pl.multiple_of(place_ref[22] * width, 128)

    def fetch(i):
        copies = []
        for k in range(4):
            source = other[(0, 2, 1, 3)[k]]
            if i == 0:
                source = own[k].at[:, pl.ds(start, width)] if k == 0 else own[k]
            rows = pl.ds(k * part, part)
            copies.append((source, weight.at[i, rows], arrived.at[i, 0, k]))
            copies.append((hidden[k].at[i], values.at[i, :, rows], arrived.at[i, 1, k]))
        return [pltpu.make_async_copy(*copy) for copy in copies]

    for i in range(2):
        for copy in fetch(i):
            copy.start()
    lanes = lax.broadcasted_iota(jnp.int32, (1, slots), 1)
    index = jnp.concatenate([low_ref[...], high_ref[...]], axis=0)
    hots = [(index[:, i : i + 1] == lanes).astype(BF16) for i in range(2)]
    for i in range(2):
        for copy in fetch(i):
            copy.wait()
        sums[i * slots : (i + 1) * slots] = jnp.dot(
            values[i], weight[i], preferred_element_type=F32
        ).astype(BF16)
    result = jnp.dot(
        jnp.concatenate(hots, axis=1), sums[...], preferred_element_type=F32
    ).astype(BF16)
    for i in range(4):
        at = pl.multiple_of(place_ref[16 + i] * 128, 128)
        out_ref[pl.ds(at, 128), :] = result[i * 128 : (i + 1) * 128]


def down(place, index_low, index_high, hidden, own, other):
    half = index_low.shape[0]
    slots, part = hidden[0].shape[1:]
    width = own[1].shape[1]
    whole = lambda *shape: pl.BlockSpec(shape, lambda i, s: (0,) * len(shape))
    return pl.pallas_call(
        down_kernel,
        grid_spec=pltpu.PrefetchScalarGridSpec(
            num_scalar_prefetch=1,
            grid=(1,),
            in_specs=[whole(half, 2)] * 2 + [pl.BlockSpec(memory_space=pl.ANY)] * 12,
            out_specs=whole(2 * half, width),
            scratch_shapes=[
                pltpu.VMEM((2, slots, 4 * part), BF16),
                pltpu.VMEM((2, 4 * part, width), BF16),
                pltpu.VMEM((2 * slots, width), BF16),
                pltpu.SemaphoreType.DMA((2, 2, 4)),
            ],
        ),
        out_shape=jax.ShapeDtypeStruct((2 * half, width), BF16),
        cost_estimate=pl.CostEstimate(
            flops=24 * half * part * width, bytes_accessed=16 * part * width, transcendentals=0
        ),
        compiler_params=pltpu.CompilerParams(vmem_limit_bytes=32 << 20),
    )(place, index_low, index_high, *hidden, *own, *other)


def per_device(
    residual,
    query_latent,
    query_rope,
    cache_latent,
    cache_rope,
    new_latent,
    new_rope,
    lengths,
    value_proj,
    out_proj,
    norm_gain,
    expert_ids,
    expert_gates,
    w_gate,
    w_up,
    w_down,
):
    rows, model = residual.shape
    expert = lax.axis_index("expert")
    plane = lax.axis_index("tensor")
    core = expert % 2
    chip = expert // 2
    first = jnp.where(core == 0, 1, 3)
    second = 4 - first
    pair = lambda v: (jnp.minimum(v, v ^ first), jnp.maximum(v, v ^ first))
    row, column = chip // SIDE, chip % SIDE
    table = []
    for far_y in range(2):
        for far_x in range(2):
            for near_y in range(2):
                for near_x in range(2):
                    table.append(
                        pair(row ^ (second * far_y))[near_y] * SIDE
                        + pair(column ^ (second * far_x))[near_x]
                    )
    for far_z in range(2):
        for near_z in range(2):
            table.append(pair(plane ^ (second * far_z))[near_z])
    is_high = lambda v: jnp.where(v == pair(v)[1], 1, 0)
    table += [chip, core, plane, is_high(row) * 2 + is_high(column), is_high(plane)]
    place = jnp.stack([jnp.asarray(v, jnp.int32) for v in table])

    quarter = model // SIDE
    half = w_down.shape[1]
    cut = lambda v, z: lax.dynamic_slice(v, (0, z * quarter), (half, quarter))
    lengths, passed, near = lax.optimization_barrier(
        (lengths, cut(w_down[0], plane ^ first ^ second), cut(w_down[0], plane ^ first))
    )
    passed, near = exchange(passed, "z", 0), exchange(near, "z", 0)
    out_other = swap_core(out_proj.T)
    gate_own, up_own = w_gate[0], w_up[0]
    gate_other, up_other = swap_core(gate_own), swap_core(up_own)

    heads = attention_heads(
        query_latent,
        query_rope,
        cache_latent,
        cache_rope,
        new_latent,
        new_rope,
        lengths,
        value_proj,
    )
    cols = model // CHIPS
    sent = pack(heads, residual, expert_ids, expert_gates)
    sent, out_other, gate_other, up_other, passed, late_down = lax.optimization_barrier(
        (sent, out_other, gate_other, up_other, passed, w_down[0])
    )
    here = cut(late_down, plane)
    far = exchange(cut(late_down, plane ^ second), "z", 1)
    lane_plane = [
        [expert_of(y, x, core) for y in range(SIDE) for x in range(SIDE)] for core in range(2)
    ]
    landed = lax.all_to_all(
        sent, "expert", split_axis=0, concat_axis=0, tiled=True, axis_index_groups=lane_plane
    )
    landed, near, far = lax.optimization_barrier((landed, near, far))
    block = project(
        jnp.stack([core, chip]).astype(jnp.int32),
        landed.reshape(CHIPS * rows, -1),
        out_proj,
        out_other.T,
        norm_gain,
    )
    last = exchange(passed, "z", 1)
    cubes = [
        [expert_of(y, x, core) * SIDE + z for z in z_pair for y in y_pair for x in x_pair]
        for core in range(2)
        for z_pair in pairs_of(core)
        for y_pair in pairs_of(core)
        for x_pair in pairs_of(core)
    ]
    block = lax.all_to_all(
        block, BOTH, split_axis=0, concat_axis=0, tiled=True, axis_index_groups=cubes
    )
    block, last = lax.optimization_barrier((block.reshape(-1, block.shape[-1]), last))
    others = [swap_core(v) for v in (here, near, far, last)]
    weights = (gate_own, gate_other, up_own, up_other)
    all_rows = ((0, 1024),)
    by_x, by_y, by_z = exchange(block, "x", 1), exchange(block, "y", 1), exchange(block, "z", 1)
    carried = gather_products(place, ((all_rows, 0, 0),), (block,), weights, None)
    own, on_x = lax.optimization_barrier((carried[1], by_x))
    own, on_y = lax.optimization_barrier((own, by_y))
    own, on_z, *others[:2] = lax.optimization_barrier((own, by_z, *others[:2]))
    carried = (carried[0], own)
    by_xy, by_yz, by_xz = exchange(on_x, "y", 1), exchange(on_y, "z", 1), exchange(on_z, "x", 1)
    carried = gather_products(
        place,
        ((all_rows, 1, 0), (all_rows, 2, 0), (all_rows, 0, 1)),
        (by_x, by_y, by_z),
        weights,
        carried,
    )
    cuts = [value[low:high] for value, (low, high) in zip((by_xy, by_yz), HALVES)]
    own, cuts[0] = lax.optimization_barrier((carried[1], cuts[0]))
    own, cuts[1], others[2], others[3] = lax.optimization_barrier(
        (own, cuts[1], others[2], others[3])
    )
    carried = (carried[0], own)
    halves = [exchange(value, axis, 1) for value, axis in zip(cuts, "zx")]
    total, own, part_sums, index_low = gather_products(
        place,
        ((all_rows, 3, 0), (all_rows, 2, 1), (all_rows, 1, 1)),
        (by_xy, by_yz, by_xz),
        weights,
        carried,
        0,
    )
    hidden, index_high = gather_products(
        place, ((HALVES, 3, 1),), tuple(halves), weights, (total, part_sums), 1
    )
    spread = [hidden, exchange(hidden, "z", 0), exchange(hidden, "z", 1), shift_z(hidden, 2)]
    sums = down(place, index_low, index_high, spread, (w_down[0], near, far, last), others)
    lane_all = [
        [expert_of(y, x, core) * SIDE + z for z in range(SIDE) for y in range(SIDE) for x in range(SIDE)]
        for core in range(2)
    ]
    returned = lax.all_to_all(
        sums.reshape(SIDE * CHIPS, rows, quarter),
        BOTH,
        split_axis=0,
        concat_axis=0,
        tiled=True,
        axis_index_groups=lane_all,
    )
    routed = jnp.sum(returned.reshape(SIDE, CHIPS, rows, quarter).astype(F32), axis=1)
    routed = routed.transpose(1, 0, 2).reshape(rows, model)
    stream = own[:, :, :cols].transpose(1, 0, 2).reshape(rows, model) / norm_gain.astype(F32)
    return (stream + routed).astype(BF16)


def solution(mesh):
    return jax.shard_map(
        per_device,
        mesh=mesh,
        in_specs=(
            P(BOTH, None),
            P(BOTH, None, None, None),
            P(BOTH, None, None, None),
            P(BOTH, None, None),
            P(BOTH, None, None),
            P(BOTH, None, None),
            P(BOTH, None, None),
            P(BOTH),
            P(),
            P(None, "expert"),
            P(),
            P(BOTH, None),
            P(BOTH, None),
            P("expert", None, "tensor"),
            P("expert", None, "tensor"),
            P("expert", "tensor", None),
        ),
        out_specs=P(BOTH, None),
        check_vma=False,
    )
```

```python
import functools

import jax
import jax.numpy as jnp
from jax import lax
from jax.experimental import pallas as pl
from jax.experimental.pallas import tpu as pltpu
from jax.sharding import PartitionSpec as P

EPSILON = 1e-06
BOTH = ("expert", "tensor")
SIDE = 4
CHIPS = 16
HALVES = ((0, 512), (512, 1024))
F32 = jnp.float32
BF16 = jnp.bfloat16


def expert_of(y, x, core):
    return (y * SIDE + x) * 2 + core


def masks_of(core):
    return (1, 3) if core == 0 else (3, 1)


def swap_core(value):
    pairs = [(e, e ^ 1) for e in range(2 * CHIPS)]
    return lax.ppermute(value, "expert", pairs)


def shift_z(value, amount):
    pairs = [(z, (z + amount) % SIDE) for z in range(SIDE)]
    return lax.ppermute(value, "tensor", pairs)


def exchange(value, axis, turn):
    pairs = []
    for y in range(SIDE):
        for x in range(SIDE):
            for core in range(2):
                mask = masks_of(core)[1 - turn if axis == "y" else turn]
                here = expert_of(y, x, core)
                if axis == "x":
                    pairs.append((here, expert_of(y, x ^ mask, core)))
                elif axis == "y":
                    pairs.append((here, expert_of(y ^ mask, x, core)))
                else:
                    for z in range(SIDE):
                        pairs.append((here * SIDE + z, here * SIDE + (z ^ mask)))
    return lax.ppermute(value, BOTH if axis == "z" else "expert", pairs)


def pairs_of(core, turn):
    mask = masks_of(core)[turn]
    return [(v, v ^ mask) for v in range(SIDE) if v < v ^ mask]


def attend_kernel(length_ref, q_ref, qr_ref, latent_ref, rope_ref, fresh_ref, fresh_rope_ref, out_ref, *, scale, heads):
    request = pl.program_id(0)
    query = q_ref[0]
    query_rope = qr_ref[0]
    latent = latent_ref[0]
    last = (((1,), (1,)), ((), ()))
    scores = lax.dot_general(query, latent, last, preferred_element_type=F32)
    scores = scores + jnp.dot(query_rope, rope_ref[0], preferred_element_type=F32)
    lane = lax.broadcasted_iota(jnp.int32, (1, scores.shape[1]), 1)
    scores = jnp.where(lane < length_ref[request], scores * scale, -1e30)
    fresh = fresh_ref[0]
    fresh_rope = fresh_rope_ref[0]
    recent = lax.dot_general(query, fresh, last, preferred_element_type=F32)
    recent = recent + lax.dot_general(query_rope, fresh_rope, last, preferred_element_type=F32)
    step = lax.broadcasted_iota(jnp.int32, recent.shape, 0) // heads
    place = lax.broadcasted_iota(jnp.int32, recent.shape, 1)
    recent = jnp.where(place <= step, recent * scale, -1e30)
    top = jnp.maximum(
        jnp.max(scores, axis=1, keepdims=True), jnp.max(recent, axis=1, keepdims=True)
    )
    weights = jnp.exp(scores - top)
    recent = jnp.exp(recent - top)
    total = jnp.sum(weights, axis=1, keepdims=True) + jnp.sum(recent, axis=1, keepdims=True)
    share = 1.0 / total
    mixed = jnp.dot((weights * share).astype(BF16), latent, preferred_element_type=F32)
    recent = (recent * share).astype(BF16).astype(F32)
    for n in range(fresh.shape[0]):
        mixed = mixed + recent[:, n : n + 1] * fresh[n : n + 1].astype(F32)
    out_ref[0] = mixed.astype(BF16)


def attention_heads(
    query_latent, query_rope, cache_latent, cache_rope, new_latent, new_rope, lengths, value_proj
):
    requests, steps, heads, latent = query_latent.shape
    rope = query_rope.shape[3]
    context = cache_latent.shape[1]
    rows = steps * heads
    scale = (value_proj.shape[2] + rope) ** (-0.5)
    whole = lambda *shape: pl.BlockSpec((1,) + shape, lambda i, s: (i, 0, 0))
    mixed = pl.pallas_call(
        functools.partial(attend_kernel, scale=scale, heads=heads),
        grid_spec=pltpu.PrefetchScalarGridSpec(
            num_scalar_prefetch=1,
            grid=(requests,),
            in_specs=[
                whole(rows, latent),
                whole(rows, rope),
                whole(context, latent),
                whole(rope, context),
                whole(steps, latent),
                whole(steps, rope),
            ],
            out_specs=whole(rows, latent),
        ),
        out_shape=jax.ShapeDtypeStruct((requests, rows, latent), BF16),
        cost_estimate=pl.CostEstimate(
            flops=2 * requests * rows * context * (2 * latent + rope),
            bytes_accessed=2 * requests * context * (latent + rope),
            transcendentals=requests * rows * context,
        ),
        compiler_params=pltpu.CompilerParams(vmem_limit_bytes=56 << 20),
    )(
        lengths,
        query_latent.reshape(requests, rows, latent),
        query_rope.reshape(requests, rows, rope),
        cache_latent,
        cache_rope,
        new_latent,
        new_rope,
    )
    head_values = jnp.einsum(
        "rshl,hlv->hrsv",
        mixed.reshape(requests, steps, heads, latent),
        value_proj,
        preferred_element_type=F32,
    )
    return head_values.astype(BF16).reshape(heads, requests * steps, -1)


def pack_kernel(heads_ref, residual_ref, ids_ref, gates_ref, out_ref):
    heads, rows, each = heads_ref.shape
    width = heads * each
    cols = residual_ref.shape[1] // CHIPS
    values = jnp.concatenate([heads_ref[head] for head in range(heads)], axis=1)
    lane = lax.broadcasted_iota(jnp.int32, (rows, 128), 1)
    gates = jnp.zeros((rows, 128), F32)
    named = jnp.zeros((rows, 128), F32)
    for k in range(ids_ref.shape[1]):
        match = ids_ref[:, k : k + 1] == lane
        gates = gates + jnp.where(match, gates_ref[:, k : k + 1], 0.0)
        named = named + jnp.where(match, 1.0, 0.0)
    above = lax.broadcasted_iota(jnp.int32, (rows, rows), 1)
    below = above < lax.broadcasted_iota(jnp.int32, (rows, rows), 0)
    below = jnp.where(below, 1.0, 0.0).astype(BF16)
    rank = jnp.dot(below, named.astype(BF16), preferred_element_type=F32)
    rank = jnp.where(named > 0.5, rank, 8.0)
    high = gates.astype(BF16).astype(F32)
    low = gates - high
    for chip in range(CHIPS):
        at = 128 - 2 * chip
        picked = jnp.where(
            lane < 2,
            pltpu.roll(high, at % 128, 1),
            jnp.where(
                lane < 4, pltpu.roll(low, (at + 2) % 128, 1), pltpu.roll(rank, (at + 4) % 128, 1)
            ),
        )
        picked = jnp.where(lane < 6, picked, 0.0)[:, : 512 - cols]
        part = residual_ref[:, chip * cols : (chip + 1) * cols]
        out_ref[chip, :, :width] = values
        out_ref[chip, :, width:] = jnp.concatenate([part, picked.astype(BF16)], axis=1)


def pack(heads, residual, ids, gates):
    count, rows, each = heads.shape
    width = count * each
    return pl.pallas_call(
        pack_kernel,
        in_specs=[pl.BlockSpec(memory_space=pltpu.VMEM)] * 4,
        out_specs=pl.BlockSpec(memory_space=pltpu.VMEM),
        out_shape=jax.ShapeDtypeStruct((CHIPS, rows, width + 512), BF16),
        cost_estimate=pl.CostEstimate(
            flops=0, bytes_accessed=2 * CHIPS * rows * (width + 512), transcendentals=0
        ),
    )(heads, residual, ids, gates)


def project_kernel(
    place_ref, in_ref, own_ref, other_ref, gain_ref, out_ref, sum_own, sum_other, *, width
):
    step = pl.program_id(0)
    depth = own_ref.shape[0]

    @pl.when(step == 0)
    def _():
        sum_own[...] = jnp.zeros_like(sum_own)
        sum_other[...] = jnp.zeros_like(sum_other)

    heads = in_ref[:, pl.ds(pl.multiple_of(step * depth, 128), depth)]
    sum_own[...] += jnp.dot(heads, own_ref[...], preferred_element_type=F32)
    sum_other[...] += jnp.dot(heads, other_ref[...], preferred_element_type=F32)

    @pl.when(step == pl.num_programs(0) - 1)
    def _():
        first = place_ref[0] == 0
        own, other = sum_own[...], sum_other[...]
        left = jnp.where(first, own, other)
        right = jnp.where(first, other, own)
        both = jnp.concatenate([left, right], axis=1).astype(BF16).astype(F32)
        tail = in_ref[:, width:].astype(F32)
        cols = both.shape[1]
        stream = tail[:, :cols] + both
        square = jnp.sum(stream * stream, axis=1, keepdims=True)
        high = square.astype(BF16).astype(F32)
        low = square - high
        extra = tail[:, cols:]
        lane = lax.broadcasted_iota(jnp.int32, extra.shape, 1)
        extra = jnp.where(lane == 6, high, jnp.where(lane == 7, low, extra))
        stream = stream * gain_ref[0].astype(F32)
        value = jnp.concatenate([stream, extra], axis=1).astype(BF16)
        for i in range(out_ref.shape[0]):
            out_ref[i] = value


def project(place, landed, own, other, gain):
    rows, total = landed.shape
    width, cols = own.shape
    steps = 4
    depth = width // steps
    out = total - width
    return pl.pallas_call(
        functools.partial(project_kernel, width=width),
        grid_spec=pltpu.PrefetchScalarGridSpec(
            num_scalar_prefetch=1,
            grid=(steps,),
            in_specs=[
                pl.BlockSpec((rows, total), lambda i, s: (0, 0)),
                pl.BlockSpec((depth, cols), lambda i, s: (i, 0)),
                pl.BlockSpec((depth, cols), lambda i, s: (i, 0)),
                pl.BlockSpec((1, 1, 2 * cols), lambda i, s: (s[1], 0, 0)),
            ],
            out_specs=pl.BlockSpec((8, rows, out), lambda i, s: (0, 0, 0)),
            scratch_shapes=[pltpu.VMEM((rows, cols), F32)] * 2,
        ),
        out_shape=jax.ShapeDtypeStruct((8, rows, out), BF16),
        cost_estimate=pl.CostEstimate(
            flops=4 * rows * width * cols, bytes_accessed=4 * width * cols, transcendentals=0
        ),
        compiler_params=pltpu.CompilerParams(vmem_limit_bytes=24 << 20),
    )(place, landed, own, other, gain.reshape(CHIPS, 1, 2 * cols))


def gather_kernel(place_ref, *refs, units, first, done, model):
    counts = [len(rows) for rows, _, _ in units]
    blocks, refs = refs[: sum(counts)], refs[sum(counts) :]
    sources, refs = refs[:4], refs[4:]
    final = done == 1
    if final:
        total_in, sums_in, hidden_ref, index_ref, total, tokens, weight, arrived = refs
    else:
        if not first:
            (total_in, own_in), refs = refs[:2], refs[2:]
        total, own_ref, refs = refs[0], refs[1], refs[2:]
        if done == 0:
            (sums_ref, index_ref), refs = refs[:2], refs[2:]
        tokens, weight, arrived = refs
    part = sources[0].shape[1]
    cols = model // CHIPS
    wide = blocks[0].shape[1]
    width = 4 * part
    spare = wide - cols

    def fetch(unit, near):
        chip = place_ref[units[unit][1] * 4 + near]
        source = pl.ds(pl.multiple_of(chip * cols, 64), cols)
        return [
            pltpu.make_async_copy(
                ref.at[source],
                weight.at[unit, pl.ds(near * wide, cols), pl.ds(i * part, part)],
                arrived.at[unit, near, i],
            )
            for i, ref in enumerate(sources)
        ]

    for unit in range(len(units)):
        for near in range(4):
            for copy in fetch(unit, near):
                copy.start()
    for unit in range(len(units)):
        for near in range(4):
            weight[unit, near * wide + cols : (near + 1) * wide] = jnp.zeros((spare, width), BF16)
    if first:
        total[...] = jnp.zeros_like(total)
        own_ref[...] = jnp.zeros_like(own_ref)
    elif final:
        total[1] = total_in[1]
    else:
        total[...] = total_in[...]
        own_ref[...] = own_in[...]

    chip = place_ref[20]
    start = pl.multiple_of(place_ref[24] * 128 + (chip // 2) * 16, 16)
    for unit, (rows, far, far_z) in enumerate(units):
        here, blocks = blocks[: len(rows)], blocks[len(rows) :]
        for (low, high), ref in zip(rows, here):
            row = low
            while row < high:
                count = min(128 - row % 128, high - row)
                near_z, near = divmod(row // 128, 4)
                at = near_z * 128 + row % 128
                tokens[at : at + count, near * wide : (near + 1) * wide] = ref[
                    row - low : row - low + count
                ]
                row += count
        extra = None
        for near in range(4):
            term = tokens[:, near * wide + cols : (near + 1) * wide].astype(F32)
            extra = term if extra is None else extra + term
            if far_z == 0:
                mine = tokens[pl.ds(start, 16), near * wide : (near + 1) * wide].astype(F32)
                own_ref[pl.ds(place_ref[far * 4 + near], 1)] = jnp.where(
                    lax.rem(chip, 2) == 0, mine[:8], mine[8:]
                )[None]
            for copy in fetch(unit, near):
                copy.wait()
        if far == 0:
            at = pl.multiple_of(place_ref[23] * wide + cols // 128 * 128, 128)
            total[far_z, :, width + spare :] = tokens[:, pl.ds(at, 128)][:, cols % 128 :].astype(
                F32
            )
        total[far_z, :, width : width + spare] += extra
        total[far_z, :, :width] += jnp.dot(
            tokens[...], weight[unit], preferred_element_type=F32
        )
    if done is None:
        return

    group = lax.broadcasted_iota(jnp.int32, (128, 1), 0) // 8
    slots = 4 * 4 * CHIPS
    lanes = lax.broadcasted_iota(jnp.int32, (1, slots), 1)
    even = place_ref[21] == 0
    extra = total[done, :, width:]
    square = (extra[:, 6:7] + extra[:, 7:8]) * (1.0 / model)
    inverse = lax.rsqrt(square + EPSILON)
    names = extra[:, spare:]
    bases = jnp.concatenate(
        [group * 4 + place_ref[16 + done * 2 + i] * (4 * CHIPS) for i in range(2)], axis=0
    )
    gates = [names[:, i : i + 1] + names[:, 2 + i : 3 + i] for i in range(2)]
    ranks = [names[:, 4 + i : 5 + i].astype(jnp.int32) for i in range(2)]
    for i in range(2):
        gate = total[done, :, i * part : (i + 1) * part] * inverse
        up = total[done, :, (2 + i) * part : (3 + i) * part] * inverse
        share = jnp.where(even, gates[i], gates[1 - i])
        rank = jnp.where(even, ranks[i], ranks[1 - i])
        value = gate * (1.0 / (1.0 + jnp.exp(-gate))) * up * share
        place_index = jnp.where(rank < 4, bases + rank, -1)
        index_ref[:, i : i + 1] = place_index
        hot = (place_index == lanes).astype(BF16)
        term = lax.dot_general(
            hot, value.astype(BF16), (((0,), (0,)), ((), ())), preferred_element_type=F32
        )
        if final:
            hidden_ref[i] = (sums_in[i] + term).astype(BF16)
        else:
            sums_ref[i] = term


def gather_products(place, units, blocks, weights, carried, done=None):
    model, part = weights[0].shape
    wide = blocks[0].shape[1]
    width = 4 * part
    tok = SIDE * 128
    spare = wide - model // CHIPS
    whole = lambda *shape: pl.BlockSpec(shape, lambda i, s: (0,) * len(shape))
    total_shape = (2, tok // 2, width + 2 * spare)
    own_shape = (CHIPS, 8, wide)
    scratch = [
        pltpu.VMEM((tok // 2, 4 * wide), BF16),
        pltpu.VMEM((len(units), 4 * wide, width), BF16),
        pltpu.SemaphoreType.DMA((len(units), 4, 4)),
    ]
    sums_shape = (2, tok // 2, part)
    index_out = ((tok // 2, 2), jnp.int32)
    carried_shapes = (total_shape, own_shape)
    if done == 1:
        outs = [(sums_shape, BF16), index_out]
        scratch = [pltpu.VMEM(total_shape, F32)] + scratch
        carried_shapes = (total_shape, sums_shape)
    else:
        outs = [(total_shape, F32), (own_shape, F32)]
        if done == 0:
            outs += [(sums_shape, F32), index_out]
    return pl.pallas_call(
        functools.partial(
            gather_kernel, units=units, first=carried is None, done=done, model=model
        ),
        grid_spec=pltpu.PrefetchScalarGridSpec(
            num_scalar_prefetch=1,
            grid=(1,),
            in_specs=[whole(*b.shape) for b in blocks]
            + [pl.BlockSpec(memory_space=pltpu.HBM)] * 4
            + ([] if carried is None else [whole(*shape) for shape in carried_shapes]),
            out_specs=[whole(*shape) for shape, _ in outs],
            scratch_shapes=scratch,
        ),
        out_shape=[jax.ShapeDtypeStruct(shape, kind) for shape, kind in outs],
        cost_estimate=pl.CostEstimate(
            flops=len(units) * tok * 4 * wide * width,
            bytes_accessed=len(units) * 8 * wide * width,
            transcendentals=0,
        ),
        compiler_params=pltpu.CompilerParams(vmem_limit_bytes=44 << 20),
    )(place, *blocks, *weights, *(() if carried is None else carried))


def down_kernel(place_ref, low_ref, high_ref, *refs):
    hidden, own, other = refs[:4], refs[4:8], refs[8:12]
    out_ref, values, weight, sums, arrived = refs[12:]
    slots = values.shape[1]
    width = weight.shape[2]
    part = weight.shape[1] // 4
    start = pl.multiple_of(place_ref[22] * width, 128)

    def fetch(i):
        copies = []
        for k in range(4):
            source = other[(0, 2, 1, 3)[k]]
            if i == 0:
                source = own[k].at[:, pl.ds(start, width)] if k == 0 else own[k]
            rows = pl.ds(k * part, part)
            copies.append((source, weight.at[i, rows], arrived.at[i, 0, k]))
            copies.append((hidden[k].at[i], values.at[i, :, rows], arrived.at[i, 1, k]))
        return [pltpu.make_async_copy(*copy) for copy in copies]

    for i in range(2):
        for copy in fetch(i):
            copy.start()
    lanes = lax.broadcasted_iota(jnp.int32, (1, slots), 1)
    index = jnp.concatenate([low_ref[...], high_ref[...]], axis=0)
    hots = [(index[:, i : i + 1] == lanes).astype(BF16) for i in range(2)]
    for i in range(2):
        for copy in fetch(i):
            copy.wait()
        sums[i * slots : (i + 1) * slots] = jnp.dot(
            values[i], weight[i], preferred_element_type=F32
        ).astype(BF16)
    result = jnp.dot(
        jnp.concatenate(hots, axis=1), sums[...], preferred_element_type=F32
    ).astype(BF16)
    for i in range(4):
        at = pl.multiple_of(place_ref[16 + i] * 128, 128)
        out_ref[pl.ds(at, 128), :] = result[i * 128 : (i + 1) * 128]


def down(place, index_low, index_high, hidden, own, other):
    half = index_low.shape[0]
    slots, part = hidden[0].shape[1:]
    width = own[1].shape[1]
    whole = lambda *shape: pl.BlockSpec(shape, lambda i, s: (0,) * len(shape))
    return pl.pallas_call(
        down_kernel,
        grid_spec=pltpu.PrefetchScalarGridSpec(
            num_scalar_prefetch=1,
            grid=(1,),
            in_specs=[whole(half, 2)] * 2 + [pl.BlockSpec(memory_space=pl.ANY)] * 12,
            out_specs=whole(2 * half, width),
            scratch_shapes=[
                pltpu.VMEM((2, slots, 4 * part), BF16),
                pltpu.VMEM((2, 4 * part, width), BF16),
                pltpu.VMEM((2 * slots, width), BF16),
                pltpu.SemaphoreType.DMA((2, 2, 4)),
            ],
        ),
        out_shape=jax.ShapeDtypeStruct((2 * half, width), BF16),
        cost_estimate=pl.CostEstimate(
            flops=24 * half * part * width, bytes_accessed=16 * part * width, transcendentals=0
        ),
        compiler_params=pltpu.CompilerParams(vmem_limit_bytes=32 << 20),
    )(place, index_low, index_high, *hidden, *own, *other)


def per_device(
    residual,
    query_latent,
    query_rope,
    cache_latent,
    cache_rope,
    new_latent,
    new_rope,
    lengths,
    value_proj,
    out_proj,
    norm_gain,
    expert_ids,
    expert_gates,
    w_gate,
    w_up,
    w_down,
):
    rows, model = residual.shape
    expert = lax.axis_index("expert")
    plane = lax.axis_index("tensor")
    core = expert % 2
    chip = expert // 2
    first = jnp.where(core == 0, 1, 3)
    second = 4 - first
    pair = lambda v, mask: (jnp.minimum(v, v ^ mask), jnp.maximum(v, v ^ mask))
    row, column = chip // SIDE, chip % SIDE
    table = []
    for far_y in range(2):
        for far_x in range(2):
            for near_y in range(2):
                for near_x in range(2):
                    table.append(
                        pair(row ^ (first * far_y), second)[near_y] * SIDE
                        + pair(column ^ (second * far_x), first)[near_x]
                    )
    for far_z in range(2):
        for near_z in range(2):
            table.append(pair(plane ^ (second * far_z), first)[near_z])
    is_high = lambda v, mask: jnp.where(v == pair(v, mask)[1], 1, 0)
    spot = is_high(row, second) * 2 + is_high(column, first)
    table += [chip, core, plane, spot, is_high(plane, first)]
    place = jnp.stack([jnp.asarray(v, jnp.int32) for v in table])

    quarter = model // SIDE
    half = w_down.shape[1]
    cut = lambda v, z: lax.dynamic_slice(v, (0, z * quarter), (half, quarter))
    lengths, passed, near = lax.optimization_barrier(
        (lengths, cut(w_down[0], plane ^ first ^ second), cut(w_down[0], plane ^ first))
    )
    passed, near = exchange(passed, "z", 0), exchange(near, "z", 0)
    out_other = swap_core(out_proj.T)
    gate_own, up_own = w_gate[0], w_up[0]
    gate_other, up_other = swap_core(gate_own), swap_core(up_own)

    heads = attention_heads(
        query_latent,
        query_rope,
        cache_latent,
        cache_rope,
        new_latent,
        new_rope,
        lengths,
        value_proj,
    )
    cols = model // CHIPS
    sent = pack(heads, residual, expert_ids, expert_gates)
    sent, out_other, gate_other, up_other, passed, late_down = lax.optimization_barrier(
        (sent, out_other, gate_other, up_other, passed, w_down[0])
    )
    here = cut(late_down, plane)
    far = exchange(cut(late_down, plane ^ second), "z", 1)
    lane_plane = [
        [expert_of(y, x, core) for y in range(SIDE) for x in range(SIDE)] for core in range(2)
    ]
    landed = lax.all_to_all(
        sent, "expert", split_axis=0, concat_axis=0, tiled=True, axis_index_groups=lane_plane
    )
    landed, near, far = lax.optimization_barrier((landed, near, far))
    block = project(
        jnp.stack([core, chip]).astype(jnp.int32),
        landed.reshape(CHIPS * rows, -1),
        out_proj,
        out_other.T,
        norm_gain,
    )
    last = exchange(passed, "z", 1)
    cubes = [
        [expert_of(y, x, core) * SIDE + z for z in z_pair for y in y_pair for x in x_pair]
        for core in range(2)
        for z_pair in pairs_of(core, 0)
        for y_pair in pairs_of(core, 1)
        for x_pair in pairs_of(core, 0)
    ]
    block = lax.all_to_all(
        block, BOTH, split_axis=0, concat_axis=0, tiled=True, axis_index_groups=cubes
    )
    block, last = lax.optimization_barrier((block.reshape(-1, block.shape[-1]), last))
    others = [swap_core(v) for v in (here, near, far, last)]
    weights = (gate_own, gate_other, up_own, up_other)
    all_rows = ((0, 1024),)
    by_x, by_y, by_z = exchange(block, "x", 1), exchange(block, "y", 1), exchange(block, "z", 1)
    carried = gather_products(place, ((all_rows, 0, 0),), (block,), weights, None)
    own, on_x = lax.optimization_barrier((carried[1], by_x))
    own, on_y = lax.optimization_barrier((own, by_y))
    own, on_z, *others[:2] = lax.optimization_barrier((own, by_z, *others[:2]))
    carried = (carried[0], own)
    by_xy, by_yz, by_xz = exchange(on_x, "y", 1), exchange(on_y, "z", 1), exchange(on_z, "x", 1)
    carried = gather_products(
        place,
        ((all_rows, 1, 0), (all_rows, 2, 0), (all_rows, 0, 1)),
        (by_x, by_y, by_z),
        weights,
        carried,
    )
    cuts = [value[low:high] for value, (low, high) in zip((by_xy, by_yz), HALVES)]
    own, cuts[0] = lax.optimization_barrier((carried[1], cuts[0]))
    own, cuts[1], others[2], others[3] = lax.optimization_barrier(
        (own, cuts[1], others[2], others[3])
    )
    carried = (carried[0], own)
    halves = [exchange(value, axis, 1) for value, axis in zip(cuts, "zx")]
    total, own, part_sums, index_low = gather_products(
        place,
        ((all_rows, 3, 0), (all_rows, 2, 1), (all_rows, 1, 1)),
        (by_xy, by_yz, by_xz),
        weights,
        carried,
        0,
    )
    hidden, index_high = gather_products(
        place, ((HALVES, 3, 1),), tuple(halves), weights, (total, part_sums), 1
    )
    spread = [hidden, exchange(hidden, "z", 0), exchange(hidden, "z", 1), shift_z(hidden, 2)]
    sums = down(place, index_low, index_high, spread, (w_down[0], near, far, last), others)
    lane_all = [
        [expert_of(y, x, core) * SIDE + z for z in range(SIDE) for y in range(SIDE) for x in range(SIDE)]
        for core in range(2)
    ]
    returned = lax.all_to_all(
        sums.reshape(SIDE * CHIPS, rows, quarter),
        BOTH,
        split_axis=0,
        concat_axis=0,
        tiled=True,
        axis_index_groups=lane_all,
    )
    routed = jnp.sum(returned.reshape(SIDE, CHIPS, rows, quarter).astype(F32), axis=1)
    routed = routed.transpose(1, 0, 2).reshape(rows, model)
    stream = own[:, :, :cols].transpose(1, 0, 2).reshape(rows, model) / norm_gain.astype(F32)
    return (stream + routed).astype(BF16)


def solution(mesh):
    return jax.shard_map(
        per_device,
        mesh=mesh,
        in_specs=(
            P(BOTH, None),
            P(BOTH, None, None, None),
            P(BOTH, None, None, None),
            P(BOTH, None, None),
            P(BOTH, None, None),
            P(BOTH, None, None),
            P(BOTH, None, None),
            P(BOTH),
            P(),
            P(None, "expert"),
            P(),
            P(BOTH, None),
            P(BOTH, None),
            P("expert", None, "tensor"),
            P("expert", None, "tensor"),
            P("expert", "tensor", None),
        ),
        out_specs=P(BOTH, None),
        check_vma=False,
    )
```
